32 devices in a mesh: expert: 8 (over y, x, core), wshard: 4 (over z).
Axes of the slice: x: 2, y: 2, z: 4, core: 2. Of those that a mesh axis runs over, the one named last changes fastest.
Arguments:
- tokens: bfloat16 [4, 1024, 768], P('wshard', 'expert'), may hold values from -6 to 6
- gain_attn: bfloat16 [768], P('wshard'), may hold values from 0.099609375 to 1.8984375
- gain_mix: bfloat16 [768], P('wshard'), may hold values from 0.099609375 to 1.8984375
- attn_in: bfloat16 [768, 2304], P('wshard'), may hold values from -0.109375 to 0.109375
- attn_out: bfloat16 [768, 768], P('wshard'), may hold values from -0.625 to 0.625
- router: bfloat16 [768, 16], P('wshard'), may hold values from -0.15625 to 0.15625
- bias_table: bfloat16 [32, 12], P('wshard'), may hold values from -4 to 4
- expert_in: bfloat16 [16, 768, 3072], P('expert', None, 'wshard'), may hold values from -0.21875 to 0.21875
- expert_down: bfloat16 [16, 768, 3072], P('expert', None, 'wshard'), may hold values from -2.5 to 2.5
- routes: int32 [4, 1024], P('wshard', 'expert'), may hold values from 0 to 15, as said below
- buckets: int32 [2047], replicated, may hold values from 0 to 31
- out_grad: bfloat16 [4, 1024, 768], P('wshard', 'expert'), may hold values from -6 to 6
Outputs:
- result: bfloat16 [4, 1024, 768], P('wshard', 'expert')
- tokens_grad: bfloat16 [4, 1024, 768], P('wshard', 'expert')
- gain_attn_grad: float32 [768], P('wshard')
- gain_mix_grad: float32 [768], P('wshard')
- attn_in_grad: float32 [768, 2304], P('wshard')
- attn_out_grad: float32 [768, 768], P('wshard')
- router_grad: float32 [768, 16], P('wshard')
- bias_table_grad: float32 [32, 12], P('wshard')
- expert_in_grad: float32 [16, 768, 3072], P('expert', None, 'wshard')
- expert_down_grad: float32 [16, 768, 3072], P('expert', None, 'wshard')
The draws below stay inside these ranges and needn't reach their ends.
Inputs may be any that keep to these rules, and one draw needn't show every extreme that they name: `routes`: among the 128 tokens of one device no expert is chosen more than 12 times, and in every draw one expert is chosen exactly 12 times by the tokens of every device.
All inputs are finite; a program needn't handle non-finite values.
Results may differ from the reference program's by a relative error of at most 0.025.
Values may be sent and summed in bfloat16 or wider, within the bound.
No kernel may reach another device: no remote copies, remote signals or barrier semaphores. Data moves between devices by JAX's collectives and lax.ppermute only.
A program may use at most 320 MiB of HBM per device.

```python
import jax
import jax.numpy as jnp
from jax import lax

D = 768
HEADS = 12
HEAD_DIM = 64
FF = 3072
BUCKETS = 32
TOK_DEV = 128
EXPERTS = 16
SEQ_LEN = 1024
SEQS = 4
CAP = 12


def draw_routes(key, part):
    key = jax.random.fold_in(key, 7)
    favourite_key, others_key = jax.random.split(key)
    favourite = jax.random.randint(favourite_key, (), 0, EXPERTS).astype(jnp.int32)
    block_count = SEQS * SEQ_LEN // TOK_DEV

    def one_block(block_index):
        block_key = jax.random.fold_in(others_key, block_index)
        pick_key, order_key = jax.random.split(block_key)
        picked = jax.random.permutation(pick_key, (EXPERTS - 1) * CAP)[:TOK_DEV - CAP] // CAP
        picked = picked.astype(jnp.int32)
        picked = picked + (picked >= favourite).astype(jnp.int32)
        row_experts = jnp.concatenate([jnp.full((CAP,), favourite, jnp.int32), picked])
        return row_experts[jax.random.permutation(order_key, TOK_DEV)]
    blocks = jax.vmap(one_block)(jnp.arange(block_count, dtype=jnp.int32))
    return blocks.reshape(SEQS, SEQ_LEN).astype(jnp.int32)


def set_ends(values, key, least, top_value):
    index_at = [jax.random.randint(jax.random.fold_in(key, axis), (), 0, length) for axis, length in enumerate(values.shape)]
    longest = values.shape.index(max(values.shape))
    beside = index_at[:longest] + [(index_at[longest] + 1) % values.shape[longest]] + index_at[longest + 1:]
    return values.at[tuple(index_at)].set(least).at[tuple(beside)].set(top_value)


def shard_levels(own_key, shape, shards, low, largest):
    def one(dim, shards_of):
        heights = jax.random.uniform(jax.random.fold_in(jax.random.fold_in(own_key, 6), dim), (shards_of,), jnp.float32, low / len(shards), largest / len(shards))
        return jnp.repeat(jnp.exp(heights), shape[dim] // shards_of).reshape((-1,) + (1,) * (len(shape) - dim - 1))

    loudness = one(*shards[0])
    for cut in shards[1:]:
        loudness = loudness * one(*cut)
    return loudness


def noise(key, dims, spread, reach, cuts=(), kind=jnp.bfloat16):
    array = spread * jax.random.normal(key, dims, jnp.float32)
    if cuts:
        array = array * shard_levels(key, dims, cuts, -0.22, 0.18)
    return jnp.clip(array, -reach, reach).astype(kind)


def setup_inputs(seed: int = 0) -> dict:
    streams_of = jax.random.split(jax.random.key(seed), 13)
    return {
        "tokens": noise(streams_of[0], (SEQS, SEQ_LEN, D), 1.0, 6.0, ((0, 4), (1, 8))),
        "gain_attn": jnp.clip(1.0 + 0.18 * jax.random.normal(streams_of[1], (D,), jnp.float32), 0.099609375, 1.8984375).astype(jnp.bfloat16),
        "gain_mix": jnp.clip(1.0 + 0.18 * jax.random.normal(streams_of[2], (D,), jnp.float32), 0.099609375, 1.8984375).astype(jnp.bfloat16),
        "attn_in": noise(streams_of[3], (D, 3 * D), (4 * D) ** -0.5, 0.109375, ((0, 4),)),
        "attn_out": noise(streams_of[4], (D, D), (max(1, D * 128 // SEQ_LEN)) ** -0.5, 0.625, ((0, 4),)),
        "router": noise(streams_of[5], (D, EXPERTS), (2 * D) ** -0.5, 0.15625, ((0, 4),)),
        "bias_table": noise(streams_of[6], (BUCKETS, HEADS), 1.0, 4.0, ((0, 4),)),
        "expert_in": noise(streams_of[7], (EXPERTS, D, FF), D ** -0.5, 0.21875, ((0, 8), (2, 4))),
        "expert_down": noise(streams_of[8], (EXPERTS, D, FF), (max(1, FF // (2 * EXPERTS * EXPERTS))) ** -0.5, 2.5, ((0, 8), (2, 4))),
        "routes": draw_routes(jax.random.fold_in(streams_of[12], 71), 0),
        "buckets": set_ends(jax.random.randint(streams_of[10], (2 * SEQ_LEN - 1,), 0, BUCKETS), jax.random.fold_in(streams_of[10], 1), 0, BUCKETS - 1).astype(jnp.int32),
        "out_grad": noise(streams_of[11], (SEQS, SEQ_LEN, D), 1.0, 6.0, ((0, 4), (1, 8))),
    }


@jax.custom_vjp
def low(v):
    return lax.optimization_barrier(v.astype(jnp.bfloat16)).astype(jnp.float32)

@jax.custom_vjp
def low_back(v):
    return v

def low_keep(v):
    return (low(v), None)

def low_pass(kept, grad):
    return (grad,)

def back_keep(v):
    return (v, None)

def back_low(kept, grad):
    return (low(grad),)
low.defvjp(low_keep, low_pass)
low_back.defvjp(back_keep, back_low)
FULL_PRECISION = lax.Precision.HIGHEST

def norm_rows(values, gain):
    scale = lax.rsqrt(lax.optimization_barrier(jnp.mean(values * values, axis=-1, keepdims=True)) + 1e-06)
    return values * scale * gain

def bidirectional_offsets(values):
    return low_back(low(values))

def attention(queries, key_rows, value_rows, bias_vec):
    query_block = min(512, SEQ_LEN)
    block_count = SEQ_LEN // query_block
    positions = jnp.arange(SEQ_LEN, dtype=jnp.int32)

    def one_block(block_index):
        sequence = block_index // block_count
        first_row = block_index % block_count * query_block
        query_seq = lax.dynamic_index_in_dim(queries, sequence, 0, keepdims=False)
        query_part = lax.dynamic_slice_in_dim(query_seq, first_row, query_block, 0)
        key_seq = lax.dynamic_index_in_dim(key_rows, sequence, 0, keepdims=False)
        value_seq = lax.dynamic_index_in_dim(value_rows, sequence, 0, keepdims=False)
        row_index = (first_row + jnp.arange(query_block, dtype=jnp.int32)).astype(jnp.int32)
        offsets = (positions[None, :] - row_index[:, None] + (SEQ_LEN - 1)).astype(jnp.int32)
        bias_block = jnp.take(bias_vec, offsets, axis=1)
        scores = jnp.einsum('qhd,khd->hqk', query_part, key_seq, precision=FULL_PRECISION) + bias_block
        scores = low_back(scores)
        weights = low(jax.nn.softmax(scores, axis=-1))
        return jnp.einsum('hqk,khd->qhd', weights, value_seq, precision=FULL_PRECISION)
    blocks = lax.map(jax.checkpoint(one_block), jnp.arange(SEQS * block_count, dtype=jnp.int32))
    return blocks.reshape(SEQS, SEQ_LEN, HEADS * HEAD_DIM)

def reference(tokens, gain_attn, gain_mix, attn_in, attn_out, router, bias_table, expert_in, expert_down, routes, buckets, out_grad):
    flat_routes = routes.reshape(-1).astype(jnp.int32)
    block_total = flat_routes.shape[0] // TOK_DEV
    by_block = flat_routes.reshape(block_total, TOK_DEV)
    expert_ids = jnp.arange(EXPERTS, dtype=jnp.int32)
    counted = (by_block[:, :, None] == expert_ids[None, None, :]).astype(jnp.int32)
    slot_rank = lax.optimization_barrier(jnp.sum((jnp.cumsum(counted, axis=1) - 1) * counted, axis=2))
    block_ids = jnp.arange(block_total, dtype=jnp.int32)[:, None]
    slot_of = (by_block * (block_total * CAP) + block_ids * CAP + slot_rank).reshape(-1).astype(jnp.int32)
    chosen = flat_routes[:, None] == expert_ids[None, :]
    bucket_ids = buckets.astype(jnp.int32)

    def forward(source_rows, gain_one, gain_two, input_weight, output_weight, w_router, bias_rows, w_up, w_down):
        first_normalized = low(norm_rows(source_rows, gain_one))
        joined_heads = bidirectional_offsets(jnp.einsum('gqj,ja->gqa', first_normalized, input_weight, precision=FULL_PRECISION))
        head_shape = (SEQS, SEQ_LEN, HEADS, HEAD_DIM)
        queries = joined_heads[:, :, :D].reshape(head_shape)
        key_rows = joined_heads[:, :, D:2 * D].reshape(head_shape)
        value_rows = joined_heads[:, :, 2 * D:].reshape(head_shape)
        bias_vec = jnp.take(bias_rows, bucket_ids, axis=0).T
        mixed_rows = bidirectional_offsets(attention(queries, key_rows, value_rows, bias_vec))
        post_attention_rows = source_rows + jnp.einsum('gqj,ja->gqa', mixed_rows, output_weight, precision=FULL_PRECISION)
        normed_two = low(norm_rows(post_attention_rows, gain_two)).reshape(-1, D)
        logits = jnp.dot(normed_two, w_router, precision=FULL_PRECISION)
        router_probs = jax.nn.softmax(logits, axis=-1)
        gate_values = lax.optimization_barrier(jnp.sum(jnp.where(chosen, router_probs, 0.0), axis=1))
        sent_rows = low_back(normed_two)
        slots = jnp.zeros((EXPERTS * block_total * CAP, D), sent_rows.dtype).at[slot_of].set(sent_rows)
        slots = slots.reshape(EXPERTS, block_total * CAP, D)

        def expert_apply(pieces):
            rows_in, up_weight, down_weight = pieces
            pre_act = low_back(jnp.dot(rows_in, up_weight, precision=FULL_PRECISION))
            hidden = low(jax.nn.gelu(pre_act))
            return bidirectional_offsets(jnp.einsum('rf,df->rd', hidden, down_weight, precision=FULL_PRECISION))
        outputs = lax.map(jax.checkpoint(expert_apply), (slots, w_up, w_down)).reshape(-1, D)
        gathered = jnp.take(outputs, slot_of, axis=0)
        return post_attention_rows + (gate_values[:, None] * gathered).reshape(source_rows.shape)
    inputs = (tokens, gain_attn, gain_mix, attn_in, attn_out, router, bias_table, expert_in, expert_down)
    as_float = tuple((entry.astype(jnp.float32) for entry in inputs))
    result, pull_back = jax.vjp(forward, *as_float)
    grads_all = pull_back(out_grad.astype(jnp.float32))
    return (result.astype(jnp.bfloat16), grads_all[0].astype(jnp.bfloat16), grads_all[1], grads_all[2], grads_all[3], grads_all[4], grads_all[5], grads_all[6], grads_all[7], grads_all[8])
```

```python
import functools

import jax
import jax.numpy as jnp
from jax import lax
from jax.experimental import pallas as pl
from jax.experimental.pallas import tpu as pltpu
from jax.sharding import PartitionSpec as P

BF = jnp.bfloat16
F32 = jnp.float32
EPS = 1e-06
LANES = 128
VMEM_BYTES = 60 * 1024 * 1024
NN = (((1,), (0,)), ((), ()))
NT = (((1,), (1,)), ((), ()))
TN = (((0,), (0,)), ((), ()))


def dot(a, b, dims=NN):
    return lax.dot_general(a, b, dims, preferred_element_type=F32)


def dot_two(a, b, dims=NN):
    high = a.astype(BF)
    low = (a - high.astype(F32)).astype(BF)
    return dot(high, b, dims) + dot(low, b, dims)


def swap(x, axis, mask):
    count = lax.axis_size(axis)
    return lax.ppermute(x, axis, [(i, i ^ mask) for i in range(count)])


def tie(*groups):
    return lax.optimization_barrier(groups)


def chip_pieces(x):
    return [x] + [swap(x, "expert", mask) for mask in range(2, lax.axis_size("expert"), 2)]


def core_pieces(pieces):
    return [block for piece in pieces for block in (piece, swap(piece, "expert", 1))]


def gather_rows(x):
    count = lax.axis_size("wshard")
    mine = lax.axis_index("wshard")
    blocks = jnp.stack([x] + [swap(x, "wshard", mask) for mask in range(1, count)])
    return jnp.take(blocks, mine ^ jnp.arange(count), axis=0, mode="clip")


def weight_chunks(shard):
    rows, columns = shard.shape
    chips = lax.axis_size("expert") // 2
    if rows % (16 * chips) or columns % (2 * LANES):
        return [lax.all_gather(shard, "wshard", axis=0, tiled=True)]
    mine = lax.axis_index("expert")
    chunk = lax.dynamic_slice(
        shard,
        (mine // 2 * (rows // chips), mine % 2 * (columns // 2)),
        (rows // chips, columns // 2),
    )
    return [chunk] + [swap(chunk, "wshard", mask) for mask in range(1, lax.axis_size("wshard"))]


def place_weight(pieces, target, expert_id, shard_id, shards):
    if len(pieces) == 1:
        target[...] = pieces[0][...]
        return
    rows, columns = target.shape
    chips = len(pieces) // 2
    chunk = rows // shards // chips
    for mask, piece in enumerate(pieces):
        source = expert_id ^ mask
        column = pl.multiple_of(source % 2 * (columns // 2), LANES)
        for step in range(shards):
            row = (shard_id ^ step) * (rows // shards) + source // 2 * chunk
            target[pl.ds(pl.multiple_of(row, 16), chunk), pl.ds(column, columns // 2)] = piece[
                step * chunk : (step + 1) * chunk, :
            ]


def place_blocks(pieces, target, expert_id, change=None):
    for mask, piece in enumerate(pieces):
        count = piece.shape[0]
        start = pl.multiple_of((expert_id ^ mask) * count, count)
        block = piece[...]
        target[pl.ds(start, count), :] = block if change is None else change(block)


def bias_rows(window, head, rows, keys):
    row = window[pl.ds(head, 1), :]
    width = row.shape[1]
    spread = jnp.broadcast_to(row, (rows, width))
    return pltpu.roll(spread, width - (rows - 1), 1, stride=1, stride_axis=0)[:, :keys]


def pair_rows(block, head_dim):
    lane = lax.broadcasted_iota(jnp.int32, block.shape, 1)
    zero = jnp.zeros_like(block)
    return jnp.concatenate(
        [jnp.where(lane < head_dim, block, zero), jnp.where(lane < head_dim, zero, block)], axis=0
    )


def pair_join(both, rows, head_dim):
    lane = lax.broadcasted_iota(jnp.int32, (rows, both.shape[1]), 1)
    return jnp.where(lane < head_dim, both[:rows], both[rows:])


def bucket_hot(window_ref, buckets):
    width = window_ref.shape[1]
    index = lax.broadcasted_iota(jnp.int32, (buckets, width), 0)
    return (index == window_ref[...]).astype(BF)


def whole(shape):
    return pl.BlockSpec(shape, lambda *_: (0,) * len(shape))


def call(body, args, outs, scratch=(), name=None, us=1.0):
    ids = pl.BlockSpec(memory_space=pltpu.SMEM)
    return pl.pallas_call(
        body,
        in_specs=[ids] + [pl.BlockSpec(memory_space=pltpu.VMEM)] * (len(args) - 1),
        out_specs=[pl.BlockSpec(memory_space=pltpu.VMEM)] * len(outs),
        out_shape=[jax.ShapeDtypeStruct(shape, kind) for shape, kind in outs],
        scratch_shapes=list(scratch),
        compiler_params=pltpu.CompilerParams(vmem_limit_bytes=VMEM_BYTES),
        cost_estimate=cost(us),
        name=name,
    )(*args)


def cost(us):
    return pl.CostEstimate(flops=int(us * 1e9), bytes_accessed=int(us * 1e6), transcendentals=0)


def normalize(block, gain):
    values = block.astype(F32)
    scale = lax.rsqrt(jnp.mean(values * values, axis=1, keepdims=True) + EPS)
    return (values * scale * gain).astype(BF)


def forward_body(sizes, *refs):
    devices, shards, heads, head_dim, buckets, in_count = sizes
    refs = list(refs)
    ids = refs.pop(0)
    tokens = [refs.pop(0) for _ in range(devices)]
    in_pieces = [refs.pop(0) for _ in range(in_count)]
    gains, table, window_ref, mirror_ref = [refs.pop(0) for _ in range(4)]
    xn_all, joined, joined_own, ext, w_in, window, mirror = refs
    expert_id = ids[0]
    shard_id = ids[1]
    rows, width = tokens[0].shape
    keys = rows * devices
    gain_one = gains[0:1, :].astype(F32)
    place_blocks(tokens, xn_all, expert_id, lambda block: normalize(block, gain_one))
    place_weight(in_pieces, w_in, expert_id, shard_id, shards)
    column_block = 2 * LANES
    row_block = min(1024, keys)

    def project(step, carry):
        row = pl.multiple_of(step // (3 * width // column_block) * row_block, row_block)
        column = pl.multiple_of(step % (3 * width // column_block) * column_block, column_block)
        joined[pl.ds(row, row_block), pl.ds(column, column_block)] = dot(
            xn_all[pl.ds(row, row_block), :], w_in[:, pl.ds(column, column_block)]
        ).astype(BF)
        return carry

    lax.fori_loop(0, (3 * width // column_block) * (keys // row_block), project, 0)
    window[...] = dot(table[...], bucket_hot(window_ref, buckets))
    mirror[...] = dot(table[...], bucket_hot(mirror_ref, buckets))
    own = pl.multiple_of(expert_id * rows, rows)
    joined_own[...] = joined[pl.ds(own, rows), :]
    lane = lax.broadcasted_iota(jnp.int32, (rows, LANES), 1)

    def attend(pair, masses):
        column = pl.multiple_of(pair * LANES, LANES)
        queries = pair_rows(joined_own[:, pl.ds(column, LANES)], head_dim)
        scores = dot(queries, joined[:, pl.ds(width + column, LANES)], NT)
        scores = scores + jnp.concatenate(
            [bias_rows(window, 2 * pair + k, rows, keys) for k in range(2)], axis=0
        )
        top = jnp.max(scores, axis=1, keepdims=True)
        probs = jnp.exp(scores - top)
        mass = jnp.sum(probs, axis=1, keepdims=True)
        mixed = dot(probs.astype(BF), joined[:, pl.ds(2 * width + column, LANES)]) / mass
        ext[:, pl.ds(column, LANES)] = pair_join(mixed, rows, head_dim).astype(BF)
        total = top + jnp.log(mass)
        masses = jnp.where(lane == 2 * pair, total[:rows], masses)
        return jnp.where(lane == 2 * pair + 1, total[rows:], masses)

    masses = lax.fori_loop(0, heads // 2, attend, jnp.zeros((rows, LANES), F32))
    high = masses.astype(BF).astype(F32)
    middle = (masses - high).astype(BF).astype(F32)
    low = (masses - high - middle).astype(BF).astype(F32)
    ext[:, width:] = (high + pltpu.roll(middle, 32, 1) + pltpu.roll(low, 64, 1)).astype(BF)


def route_body(sizes, *refs):
    shards, experts, out_count = sizes
    refs = list(refs)
    ids = refs.pop(0)
    out_pieces = [refs.pop(0) for _ in range(out_count)]
    tokens, ext, gains, router, chosen, slots = [refs.pop(0) for _ in range(6)]
    after, gate, send, w_out = refs
    rows, width = tokens.shape
    place_weight(out_pieces, w_out, ids[0], ids[1], shards)
    lane = lax.broadcasted_iota(jnp.int32, (rows, LANES), 1)
    post = tokens[...].astype(F32) + dot(ext[:, :width], w_out[...])
    after[...] = post
    xn_two = normalize(post, gains[1:2, :].astype(F32))
    logits = jnp.where(lane < experts, dot(xn_two, router[...]), -1e30)
    weights = jnp.exp(logits - jnp.max(logits, axis=1, keepdims=True))
    weights = weights / jnp.sum(weights, axis=1, keepdims=True)
    gate[...] = jnp.broadcast_to(
        jnp.sum(weights * chosen[...].astype(F32), axis=1, keepdims=True), (rows, LANES)
    )
    send[...] = dot(slots[...], xn_two).astype(BF)


def slot_pick(count, total, capacity, which):
    row = lax.broadcasted_iota(jnp.int32, (count, total), 0)
    column = lax.broadcasted_iota(jnp.int32, (count, total), 1)
    block = total // count * capacity
    return (column == row // capacity * block + which * capacity + row % capacity).astype(BF)


def upstream_body(sizes, *refs):
    shards, per_device, capacity = sizes
    refs = list(refs)
    chunks = [refs.pop(0) for _ in range(shards)]
    w_down, up_ref, spread_ref = refs
    total = chunks[0].shape[0]
    count = total // per_device
    pick = slot_pick(count, total, capacity, pl.program_id(0))
    for step, chunk in enumerate(chunks):
        up_ref[0, step * count : (step + 1) * count, :] = dot(pick, chunk[...]).astype(BF)
    spread_ref[0] = dot(up_ref[0], w_down[0])


def expert_body(sizes, ids, rows_in, ups_in, spread_in, w_up, router, back_ref, x_ref, up_ref, hidden_ref, pre_ref, logit_ref):
    experts, per_device, capacity = sizes
    which = pl.program_id(0)
    mine = ids[0] * per_device + which
    total = rows_in.shape[0]
    count = total // per_device
    pick = slot_pick(count, total, capacity, which)
    x = dot(pick, rows_in[...]).astype(BF)
    lane = lax.broadcasted_iota(jnp.int32, (count, LANES), 1)
    logits = jnp.where(lane < experts, dot(x, router[...]), -1e30)
    probs = jnp.exp(logits - jnp.max(logits, axis=1, keepdims=True))
    probs = probs / jnp.sum(probs, axis=1, keepdims=True)
    hot = (lane == mine).astype(F32)
    gate = jnp.sum(probs * hot, axis=1, keepdims=True)
    pre = dot(x, w_up[0])
    inner = 0.7978845608028654 * (pre + 0.044715 * pre * pre * pre)
    bend = jnp.tanh(inner)
    hidden = 0.5 * pre * (1.0 + bend)
    slope = 0.5 * (1.0 + bend) + 0.5 * pre * (1.0 - bend * bend) * (
        0.7978845608028654 * (1.0 + 3.0 * 0.044715 * pre * pre)
    )
    hidden_low = hidden.astype(BF)
    spread = spread_in[0]
    gate_part = jnp.sum(hidden_low.astype(F32) * spread, axis=1, keepdims=True)
    pre_grad = (gate * spread * slope).astype(BF)
    logit_grad = gate_part * probs * (hot - gate)
    back = dot(pre_grad, w_up[0], NT) + dot_two(logit_grad, router[...], NT)
    x_ref[0] = x
    up_ref[0] = (gate * ups_in[0].astype(F32)).astype(BF)
    hidden_ref[0] = hidden_low
    pre_ref[0] = pre_grad
    logit_ref[0] = logit_grad
    back = dot(pick, back.astype(BF), TN).astype(BF)

    @pl.when(which == 0)
    def _():
        back_ref[...] = back

    @pl.when(which > 0)
    def _():
        back_ref[...] = (back_ref[...].astype(F32) + back.astype(F32)).astype(BF)


def expert_weights_body(sizes, *refs):
    shards, per_device, capacity = sizes
    refs = list(refs)
    x, up, hidden, pre, logit = [
        jnp.concatenate([refs.pop(0)[0] for _ in range(shards)], axis=0) for _ in range(5)
    ]
    w_down = refs.pop(0)
    out_refs = [refs.pop(0) for _ in range(shards)]
    up_grad, down_grad, router_part = refs
    which = pl.program_id(0)
    down_grad[0] = dot(up, hidden, TN)
    up_grad[0] = dot(x, pre, TN)
    router_add = dot_two(logit, x, TN)
    out = dot(hidden, w_down[0], NT).astype(BF)
    count = out.shape[0] // shards
    total = count * per_device
    pick = slot_pick(count, total, capacity, which)
    parts = [dot(pick, out[m * count : (m + 1) * count], TN).astype(BF) for m in range(shards)]

    @pl.when(which == 0)
    def _():
        router_part[...] = router_add
        for ref, part in zip(out_refs, parts):
            ref[...] = part

    @pl.when(which > 0)
    def _():
        router_part[...] = router_part[...] + router_add
        for ref, part in zip(out_refs, parts):
            ref[...] = (ref[...].astype(F32) + part.astype(F32)).astype(BF)


def norm_back(values, gain, grad):
    scale = lax.rsqrt(jnp.mean(values * values, axis=1, keepdims=True) + EPS)
    unit = values * scale
    inner = grad * gain
    gain_grad = jnp.sum(grad * unit, axis=0, keepdims=True)
    return scale * (inner - unit * jnp.mean(inner * unit, axis=1, keepdims=True)), gain_grad


def residual_body(ids, returned, back_slots, after, upstream, gains, resid, resid_low, gain_part):
    grad = dot(back_slots[...], returned[...])
    value, part = norm_back(after[...], gains[1:2, :].astype(F32), grad)
    value = value + upstream[...].astype(F32)
    resid[...] = value
    resid_low[...] = value.astype(BF)
    gain_part[...] = part


def result_body(ids, returned, back_slots, after, gate, result):
    rows = dot(back_slots[...], returned[...]).astype(BF).astype(F32)
    result[...] = (after[...] + gate[:, :1] * rows).astype(BF)


def diagonal_parts(block, width):
    rows, keys = block.shape
    total = jnp.zeros((8, width), F32)
    for group in range(rows // 8):
        part = jnp.concatenate(
            [block[group * 8 : group * 8 + 8], jnp.zeros((8, width - keys), F32)], axis=1
        )
        total = total + pltpu.roll(part, rows - 8 - 8 * group, 1)
    return total


def member_rows(head_rows, width, head_dim):
    head_of = lax.broadcasted_iota(jnp.int32, (head_rows, width), 1) // head_dim
    return (head_of == lax.broadcasted_iota(jnp.int32, (head_rows, width), 0)).astype(BF)


def part_rows(head_rows):
    part_of = lax.broadcasted_iota(jnp.int32, (head_rows, LANES), 1) % 32
    return (part_of == lax.broadcasted_iota(jnp.int32, (head_rows, LANES), 0)).astype(BF)


def query_body(sizes, ids, resid_low, ext, joined_own, w_out, window, window_ref, keys_in, values_in, query_grad, table_part, grads, delta, mass, diagonals):
    head_dim, buckets = sizes
    pair = pl.program_id(0)
    rows, width = resid_low.shape
    keys = keys_in.shape[0]
    head_rows, span = window.shape

    @pl.when(pair == 0)
    def _():
        low = dot(resid_low[...], w_out[...], NT).astype(BF)
        grads[...] = low
        product = low.astype(F32) * ext[:, :width].astype(F32)
        delta[...] = dot_two(product, member_rows(head_rows, width, head_dim), NT)
        mass[...] = dot(ext[:, width:], part_rows(head_rows), NT)

    head_lane = lax.broadcasted_iota(jnp.int32, (rows, head_rows), 1)

    def column_of(ref):
        return jnp.concatenate(
            [
                jnp.sum(jnp.where(head_lane == 2 * pair + k, ref[...], 0.0), axis=1, keepdims=True)
                for k in range(2)
            ],
            axis=0,
        )

    column = pl.multiple_of(pair * LANES, LANES)
    queries = pair_rows(joined_own[:, pl.ds(column, LANES)], head_dim)
    grad_own = pair_rows(grads[:, pl.ds(column, LANES)], head_dim)
    scores = dot(queries, keys_in[...], NT) + jnp.concatenate(
        [bias_rows(window, 2 * pair + k, rows, keys) for k in range(2)], axis=0
    )
    probs = jnp.exp(scores - column_of(mass))
    score_grad = (probs * (dot(grad_own, values_in[...], NT) - column_of(delta))).astype(BF)
    query_grad[0] = pair_join(dot(score_grad, keys_in[...]), rows, head_dim).astype(BF)
    wide = score_grad.astype(F32)
    for k in range(2):
        start = pl.multiple_of((2 * pair + k) * 8, 8)
        diagonals[pl.ds(start, 8), :] = diagonal_parts(wide[k * rows : (k + 1) * rows], span)

    @pl.when(pair == pl.num_programs(0) - 1)
    def _():
        every = diagonals[...]
        total_rows = every.shape[0]
        lined = jnp.zeros((total_rows, span), F32)
        place = lax.broadcasted_iota(jnp.int32, (total_rows, span), 0) % 8
        for step in range(8):
            moved = every if step == 7 else pltpu.roll(every, 7 - step, 1)
            lined = jnp.where(place == step, moved, lined)
        line_rows = lax.broadcasted_iota(jnp.int32, (head_rows, total_rows), 1) // 8
        fold = (line_rows == lax.broadcasted_iota(jnp.int32, (head_rows, total_rows), 0)).astype(BF)
        high = lined.astype(BF)
        low = (lined - high.astype(F32)).astype(BF)
        sums = dot(fold, high) + dot(fold, low)
        table_part[...] = dot_two(sums, bucket_hot(window_ref, buckets), NT)


def key_body(sizes, *refs):
    devices, heads, head_dim = sizes
    refs = list(refs)
    ids = refs.pop(0)
    resid_pieces = [refs.pop(0) for _ in range(devices)]
    ext_pieces = [refs.pop(0) for _ in range(devices)]
    joined_own, w_out, mirror, query_grad, queries_in = [refs.pop(0) for _ in range(5)]
    blocks, mixed_all, grads, delta_rows, mass_rows, mass_all = refs
    expert_id = ids[0]
    pair = pl.program_id(0)
    rows, width = resid_pieces[0].shape
    keys = rows * devices
    head_rows = mirror.shape[0]
    pairs = heads // 2

    @pl.when(pair == 0)
    def _():
        place_blocks(resid_pieces, grads, expert_id)
        for mask, piece in enumerate(ext_pieces):
            start = pl.multiple_of((expert_id ^ mask) * rows, rows)
            mixed_all[pl.ds(start, rows), :] = piece[:, :width]
            mass_all[pl.ds(start, rows), :] = piece[:, width:]
        mass_rows[...] = dot(part_rows(head_rows), mass_all[...], NT)
        member = member_rows(head_rows, width, head_dim)
        step = min(1024, keys)
        for start in range(0, keys, step):
            low = dot(grads[start : start + step, :], w_out[...], NT).astype(BF)
            grads[start : start + step, :] = low
            product = low.astype(F32) * mixed_all[start : start + step, :].astype(F32)
            high = product.astype(BF)
            rest = (product - high.astype(F32)).astype(BF)
            delta_rows[:, start : start + step] = dot(member, high, NT) + dot(member, rest, NT)
        blocks[:pairs] = query_grad[...]
        for block in range(pairs):
            blocks[3 * pairs + block] = resid_pieces[0][:, block * LANES : (block + 1) * LANES]
        for block in range(4 * pairs, blocks.shape[0]):
            blocks[block] = jnp.zeros((rows, LANES), BF)

    def row_of(ref):
        return jnp.concatenate(
            [jnp.broadcast_to(ref[pl.ds(2 * pair + k, 1), :], (rows, keys)) for k in range(2)],
            axis=0,
        )

    column = pl.multiple_of(pair * LANES, LANES)
    grad_all = grads[:, pl.ds(column, LANES)]
    key_own = pair_rows(joined_own[:, pl.ds(width + column, LANES)], head_dim)
    value_own = pair_rows(joined_own[:, pl.ds(2 * width + column, LANES)], head_dim)
    scores = dot(key_own, queries_in[...], NT) + jnp.concatenate(
        [bias_rows(mirror, 2 * pair + k, rows, keys) for k in range(2)], axis=0
    )
    probs = jnp.exp(scores - row_of(mass_rows))
    score_grad = (probs * (dot(value_own, grad_all, NT) - row_of(delta_rows))).astype(BF)
    blocks[pairs + pair] = pair_join(dot(score_grad, queries_in[...]), rows, head_dim).astype(BF)
    blocks[2 * pairs + pair] = pair_join(dot(probs.astype(BF), grad_all), rows, head_dim).astype(BF)


def source_body(ids, blocks, w_in, tokens, gains, resid, tokens_grad, gain_part, joined):
    for block in range(joined.shape[1] // LANES):
        joined[:, block * LANES : (block + 1) * LANES] = blocks[block]
    grad = dot(joined[...], w_in[...], NT)
    value, part = norm_back(tokens[...].astype(F32), gains[0:1, :].astype(F32), grad)
    tokens_grad[...] = (value + resid[...]).astype(BF)
    gain_part[...] = part


def weight_body(per, pairs, ids, xn_all, mixed_all, received, part, columns):
    devices, _, rows, _ = received.shape
    for source in range(devices):
        for block in range(per):
            columns[source * rows : (source + 1) * rows, block * LANES : (block + 1) * LANES] = received[
                source, block
            ]
    for block in range(per):
        inside = ids[0] * per + block < 3 * pairs
        line = slice(block * LANES, (block + 1) * LANES)

        @pl.when(inside)
        def _():
            part[:, line] = dot(xn_all[...], columns[:, line], TN).astype(BF)

        @pl.when(jnp.logical_not(inside))
        def _():
            part[:, line] = dot(mixed_all[...], columns[:, line], TN).astype(BF)


def spread_body(per, pairs, ids, *refs):
    pieces, (in_grad, out_grad) = refs[:-2], refs[-2:]
    for mask, piece in enumerate(pieces):
        source = ids[0] ^ mask
        for block in range(per):
            index = source * per + block
            values = piece[:, block * LANES : (block + 1) * LANES].astype(F32)

            @pl.when(index < 3 * pairs)
            def _():
                in_grad[:, pl.ds(pl.multiple_of(index * LANES, LANES), LANES)] = values

            @pl.when(jnp.logical_and(index >= 3 * pairs, index < 4 * pairs))
            def _():
                out_grad[:, pl.ds(pl.multiple_of((index - 3 * pairs) * LANES, LANES), LANES)] = values


def pad_to(x, shape):
    return jnp.pad(x, [(0, size - have) for size, have in zip(shape, x.shape)])


def local(
    tokens, gain_attn, gain_mix, attn_in, attn_out, router, bias_table, expert_in, expert_down, routes, buckets, out_grad
):
    own_tokens = tokens[0]
    own_grad = out_grad[0]
    rows, width = own_tokens.shape
    devices = lax.axis_size("expert")
    shards = lax.axis_size("wshard")
    expert_id = lax.axis_index("expert")
    shard_id = lax.axis_index("wshard")
    heads = bias_table.shape[1]
    head_dim = width // heads
    experts = router.shape[1]
    bucket_count = bias_table.shape[0] * shards
    per_device = expert_in.shape[0]
    keys = rows * devices
    capacity = 3 * rows // (2 * experts)
    part = width // shards
    ids = jnp.stack([expert_id, shard_id]).astype(jnp.int32)

    in_chunks = weight_chunks(attn_in)
    token_pieces, in_chunks, attn_out, own_grad = tie(
        chip_pieces(own_tokens), in_chunks, attn_out, own_grad
    )
    out_chunks = weight_chunks(attn_out)
    chunked = len(in_chunks) > 1
    if chunked:
        in_pieces = chip_pieces(jnp.concatenate(in_chunks, axis=0))
    token_pieces = core_pieces(token_pieces)
    if chunked:
        in_pieces = core_pieces(in_pieces)
    else:
        in_pieces = in_chunks
    small_columns = -(-(experts + 2 + heads) // LANES) * LANES
    table_rows = bias_table.shape[0]
    small = jnp.concatenate(
        [
            router,
            gain_attn[:, None],
            gain_mix[:, None],
            pad_to(bias_table, (part, heads)),
            jnp.zeros((part, small_columns - experts - 2 - heads), BF),
        ],
        axis=1,
    )
    small = gather_rows(small)
    router_all = small[:, :, :experts].reshape(width, experts)
    router_pad = pad_to(router_all, (width, LANES))
    gains = pad_to(small[:, :, experts : experts + 2].reshape(width, 2).T, (8, width))
    table = small[:, :table_rows, experts + 2 : experts + 2 + heads].reshape(bucket_count, heads)
    head_rows = 16
    table_t = pad_to(table.T, (head_rows, bucket_count))

    window_width = keys + rows
    start = keys - 1 - expert_id * rows - (rows - 1)
    window_buckets = lax.dynamic_slice(jnp.pad(buckets, (0, rows)), (start,), (window_width,))
    mirror_buckets = lax.dynamic_slice(jnp.pad(buckets[::-1], (0, rows)), (start,), (window_width,))
    last = jnp.arange(window_width) == window_width - 1
    window_buckets = jnp.where(last, -1, window_buckets)[None]
    mirror_buckets = jnp.where(last, -1, mirror_buckets)[None]

    route = routes[0]
    earlier = jnp.arange(rows)[None, :] < jnp.arange(rows)[:, None]
    rank = jnp.sum(((route[None, :] == route[:, None]) & earlier).astype(jnp.int32), axis=1)
    slot = route * capacity + rank
    slot_count = experts * capacity
    slots = (jnp.arange(slot_count)[:, None] == slot[None, :]).astype(BF)
    back_slots = (slot[:, None] == jnp.arange(slot_count)[None, :]).astype(BF)
    chosen = (route[:, None] == jnp.arange(LANES)[None, :]).astype(BF)

    block = per_device * capacity

    def scatter_rows(parts):
        mine = lax.dynamic_index_in_dim(parts, shard_id, 0, keepdims=False).astype(F32)
        for mask in range(1, shards):
            sent = lax.dynamic_index_in_dim(parts, shard_id ^ mask, 0, keepdims=False)
            mine = mine + swap(sent, "wshard", mask).astype(F32)
        return mine

    def sum_lines(lines):
        lines = lines.reshape(lines.shape[0], shards, part).transpose(1, 0, 2)
        lines = scatter_rows(lines)
        mask = 1
        while mask < devices:
            lines = lines + swap(lines, "expert", mask)
            mask *= 2
        return lines

    def exchange(slot_rows):
        blocks = slot_rows.reshape(devices, block, width)
        moved = lax.all_to_all(blocks, "expert", split_axis=0, concat_axis=0, tiled=True)
        return moved.reshape(devices * block, width)

    def to_shards(x):
        return [x] + [swap(x, "wshard", mask) for mask in range(1, shards)]

    def sum_back(parts):
        total = parts[0].astype(F32)
        for mask in range(1, shards):
            total = total + swap(parts[mask], "wshard", mask).astype(F32)
        return total.astype(BF)

    ups, in_pieces, out_chunks = tie(
        exchange(dot(slots, own_grad).astype(BF)), in_pieces, out_chunks
    )
    ups_chunks = to_shards(ups)
    if len(out_chunks) > 1:
        out_chunks = chip_pieces(jnp.concatenate(out_chunks, axis=0))

    sizes = (devices, shards, heads, head_dim, bucket_count, len(in_pieces))
    xn_all, joined, joined_own, ext, w_in, window, mirror = call(
        functools.partial(forward_body, sizes),
        [ids, *token_pieces, *in_pieces, gains, table_t, window_buckets, mirror_buckets],
        [
            ((keys, width), BF),
            ((keys, 3 * width), BF),
            ((rows, 3 * width), BF),
            ((rows, width + LANES), BF),
            ((width, 3 * width), BF),
            ((head_rows, window_width), F32),
            ((head_rows, window_width), F32),
        ],
        name="attention_forward",
        us=18.0,
    )
    out_pieces, ext = tie(out_chunks, ext)
    if len(out_pieces) > 1:
        out_pieces = core_pieces(out_pieces)
    after, gate, send, w_out = call(
        functools.partial(route_body, (shards, experts, len(out_pieces))),
        [ids, *out_pieces, own_tokens, ext, gains, router_pad, chosen, slots],
        [
            ((rows, width), F32),
            ((rows, LANES), F32),
            ((slot_count, width), BF),
            ((width, width), BF),
        ],
        name="route",
        us=4.0,
    )
    rows_own = exchange(send)
    row_chunks = to_shards(rows_own)
    ext_later, _ = tie(ext, rows_own)
    ext_pieces = core_pieces(chip_pieces(ext_later))
    total = devices * block
    count = total // per_device
    ff = expert_in.shape[2]
    by_expert = pl.BlockSpec((1, width, ff), lambda k: (k, 0, 0))
    kept_ff = pl.BlockSpec((1, count, ff), lambda k: (k, 0, 0))
    kept_width = pl.BlockSpec((1, count, width), lambda k: (k, 0, 0))
    kept_lanes = pl.BlockSpec((1, count, LANES), lambda k: (k, 0, 0))
    upstream_width = pl.BlockSpec((1, shards * count, width), lambda k: (k, 0, 0))
    upstream_ff = pl.BlockSpec((1, shards * count, ff), lambda k: (k, 0, 0))
    ups_all, spread_all = pl.pallas_call(
        functools.partial(upstream_body, (shards, per_device, capacity)),
        grid=(per_device,),
        in_specs=[whole((total, width))] * shards + [by_expert],
        out_specs=[upstream_width, upstream_ff],
        out_shape=[
            jax.ShapeDtypeStruct((per_device, shards * count, width), BF),
            jax.ShapeDtypeStruct((per_device, shards * count, ff), F32),
        ],
        compiler_params=pltpu.CompilerParams(vmem_limit_bytes=VMEM_BYTES),
        cost_estimate=cost(5.0),
        name="upstream",
    )(*ups_chunks, expert_down)
    rows_own, ups_all, spread_all = tie(rows_own, ups_all, spread_all)
    row_chunks = [rows_own] + row_chunks[1:]
    kept = [[], [], [], [], []]
    back_parts = []
    for step, row_chunk in enumerate(row_chunks):
        back, *saved = pl.pallas_call(
            functools.partial(expert_body, (experts, per_device, capacity)),
            grid=(per_device,),
            in_specs=[
                pl.BlockSpec(memory_space=pltpu.SMEM),
                whole((total, width)),
                pl.BlockSpec((1, count, width), lambda k, step=step: (k, step, 0)),
                pl.BlockSpec((1, count, ff), lambda k, step=step: (k, step, 0)),
                by_expert,
                whole((width, LANES)),
            ],
            out_specs=[whole((total, width)), kept_width, kept_width, kept_ff, kept_ff, kept_lanes],
            out_shape=[
                jax.ShapeDtypeStruct((total, width), BF),
                jax.ShapeDtypeStruct((per_device, count, width), BF),
                jax.ShapeDtypeStruct((per_device, count, width), BF),
                jax.ShapeDtypeStruct((per_device, count, ff), BF),
                jax.ShapeDtypeStruct((per_device, count, ff), BF),
                jax.ShapeDtypeStruct((per_device, count, LANES), F32),
            ],
            compiler_params=pltpu.CompilerParams(vmem_limit_bytes=VMEM_BYTES),
            cost_estimate=cost(5.0),
            name="experts",
        )(ids, row_chunk, ups_all, spread_all, expert_in, router_pad)
        back_parts.append(back)
        for group, value in zip(kept, saved):
            group.append(value)
    returned_grad = exchange(sum_back(back_parts))
    *out_parts, up_grad, down_grad, router_part = pl.pallas_call(
        functools.partial(expert_weights_body, (shards, per_device, capacity)),
        grid=(per_device,),
        in_specs=[kept_width] * (2 * shards)
        + [kept_ff] * (2 * shards)
        + [kept_lanes] * shards
        + [by_expert],
        out_specs=[whole((total, width))] * shards + [by_expert, by_expert, whole((LANES, width))],
        out_shape=[jax.ShapeDtypeStruct((total, width), BF)] * shards
        + [
            jax.ShapeDtypeStruct((per_device, width, ff), F32),
            jax.ShapeDtypeStruct((per_device, width, ff), F32),
            jax.ShapeDtypeStruct((LANES, width), F32),
        ],
        compiler_params=pltpu.CompilerParams(vmem_limit_bytes=VMEM_BYTES),
        cost_estimate=cost(8.0),
        name="expert_weights",
    )(*[value for group in kept for value in group], expert_down)
    resid, resid_low, gain_two_part = call(
        residual_body,
        [ids, returned_grad, back_slots, after, own_grad, gains],
        [((rows, width), F32), ((rows, width), BF), ((1, width), F32)],
        name="residual",
        us=2.0,
    )
    out_sum = sum_back(out_parts)
    resid_pieces = chip_pieces(resid_low)
    pairs = heads // 2

    def column_block(offset):
        return pl.BlockSpec((keys, LANES), lambda p: (0, offset * pairs + p))

    query_grad, table_part = pl.pallas_call(
        functools.partial(query_body, (head_dim, bucket_count)),
        grid=(pairs,),
        in_specs=[
            pl.BlockSpec(memory_space=pltpu.SMEM),
            whole((rows, width)),
            whole((rows, width + LANES)),
            whole((rows, 3 * width)),
            whole((width, width)),
            whole((head_rows, window_width)),
            whole((1, window_width)),
            column_block(1),
            column_block(2),
        ],
        out_specs=[pl.BlockSpec((1, rows, LANES), lambda p: (p, 0, 0)), whole((head_rows, bucket_count))],
        out_shape=[
            jax.ShapeDtypeStruct((pairs, rows, LANES), BF),
            jax.ShapeDtypeStruct((head_rows, bucket_count), F32),
        ],
        scratch_shapes=[
            pltpu.VMEM((rows, width), BF),
            pltpu.VMEM((rows, head_rows), F32),
            pltpu.VMEM((rows, head_rows), F32),
            pltpu.VMEM((head_rows * 8, window_width), F32),
        ],
        compiler_params=pltpu.CompilerParams(vmem_limit_bytes=VMEM_BYTES),
        cost_estimate=cost(10.0),
        name="query_grad",
    )(ids, resid_low, ext, joined_own, w_out, window, window_buckets, joined, joined)
    per = -(-4 * pairs // devices)
    resid_pieces, query_grad, table_part, out_sum = tie(resid_pieces, query_grad, table_part, out_sum)
    resid_pieces = core_pieces(resid_pieces)
    returned_rows = exchange(out_sum)
    table_line = table_part[:heads].T.reshape(shards, table_rows * heads)
    table_line = pad_to(table_line, (shards, part)).reshape(1, width)
    lines = sum_lines(jnp.concatenate([router_part[:experts], gain_two_part, table_line], axis=0))
    blocks, mixed_all = pl.pallas_call(
        functools.partial(key_body, (devices, heads, head_dim)),
        grid=(pairs,),
        in_specs=[pl.BlockSpec(memory_space=pltpu.SMEM)]
        + [whole((rows, width))] * devices
        + [whole((rows, width + LANES))] * devices
        + [
            whole((rows, 3 * width)),
            whole((width, width)),
            whole((head_rows, window_width)),
            whole((pairs, rows, LANES)),
            column_block(0),
        ],
        out_specs=[whole((per * devices, rows, LANES)), whole((keys, width))],
        out_shape=[
            jax.ShapeDtypeStruct((per * devices, rows, LANES), BF),
            jax.ShapeDtypeStruct((keys, width), BF),
        ],
        scratch_shapes=[
            pltpu.VMEM((keys, width), BF),
            pltpu.VMEM((head_rows, keys), F32),
            pltpu.VMEM((head_rows, keys), F32),
            pltpu.VMEM((keys, LANES), BF),
        ],
        compiler_params=pltpu.CompilerParams(vmem_limit_bytes=VMEM_BYTES),
        cost_estimate=cost(12.0),
        name="key_grad",
    )(ids, *resid_pieces, *ext_pieces, joined_own, w_out, mirror, query_grad, joined)
    blocks, lines, returned_rows = tie(blocks, lines, returned_rows)
    received = lax.all_to_all(
        blocks.reshape(devices, per, rows, LANES), "expert", split_axis=0, concat_axis=0, tiled=True
    )
    (result,) = call(
        result_body,
        [ids, returned_rows, back_slots, after, gate],
        [((rows, width), BF)],
        name="result",
        us=2.0,
    )
    tokens_grad, gain_one_part = call(
        source_body,
        [ids, blocks, w_in, own_tokens, gains, resid],
        [((rows, width), BF), ((1, width), F32)],
        [pltpu.VMEM((rows, 3 * width), BF)],
        name="source_grad",
        us=4.0,
    )
    (weight_part,) = call(
        functools.partial(weight_body, per, pairs),
        [ids, xn_all, mixed_all, received],
        [((width, per * LANES), BF)],
        [pltpu.VMEM((keys, per * LANES), BF)],
        name="weight_grads",
        us=4.0,
    )

    mine = scatter_rows(weight_part.reshape(shards, part, per * LANES)).astype(BF)
    attn_in_grad, attn_out_grad = call(
        functools.partial(spread_body, per, pairs),
        [ids, *core_pieces(chip_pieces(mine))],
        [((part, 3 * width), F32), ((part, width), F32)],
        name="spread",
        us=2.0,
    )

    (gain_line,) = sum_lines(gain_one_part)
    router_grad = lines[:experts].T
    table_grad = lines[experts + 1, : table_rows * heads].reshape(table_rows, heads)
    return (
        result[None],
        tokens_grad[None],
        gain_line,
        lines[experts],
        attn_in_grad,
        attn_out_grad,
        router_grad,
        table_grad,
        up_grad,
        down_grad,
    )


def solution(mesh):
    return jax.shard_map(
        local,
        mesh=mesh,
        in_specs=(
            P("wshard", "expert", None),
            P("wshard"),
            P("wshard"),
            P("wshard", None),
            P("wshard", None),
            P("wshard", None),
            P("wshard", None),
            P("expert", None, "wshard"),
            P("expert", None, "wshard"),
            P("wshard", "expert"),
            P(),
            P("wshard", "expert", None),
        ),
        out_specs=(
            P("wshard", "expert", None),
            P("wshard", "expert", None),
            P("wshard"),
            P("wshard"),
            P("wshard", None),
            P("wshard", None),
            P("wshard", None),
            P("wshard", None),
            P("expert", None, "wshard"),
            P("expert", None, "wshard"),
        ),
        check_vma=False,
    )
```

```python
import functools

import jax
import jax.numpy as jnp
from jax import lax
from jax.experimental import pallas as pl
from jax.experimental.pallas import tpu as pltpu
from jax.sharding import PartitionSpec as P

BF = jnp.bfloat16
F32 = jnp.float32
EPS = 1e-06
LANES = 128
VMEM_BYTES = 60 * 1024 * 1024
NN = (((1,), (0,)), ((), ()))
NT = (((1,), (1,)), ((), ()))
TN = (((0,), (0,)), ((), ()))


def dot(a, b, dims=NN):
    return lax.dot_general(a, b, dims, preferred_element_type=F32)


def dot_two(a, b, dims=NN):
    high = a.astype(BF)
    low = (a - high.astype(F32)).astype(BF)
    return dot(high, b, dims) + dot(low, b, dims)


def swap(x, axis, mask):
    count = lax.axis_size(axis)
    return lax.ppermute(x, axis, [(i, i ^ mask) for i in range(count)])


def tie(*groups):
    return lax.optimization_barrier(groups)


def chip_pieces(x):
    return [x] + [swap(x, "expert", mask) for mask in range(2, lax.axis_size("expert"), 2)]


def core_pieces(pieces):
    return [block for piece in pieces for block in (piece, swap(piece, "expert", 1))]


def weight_chunks(shard, small):
    rows, columns = shard.shape
    chips = lax.axis_size("expert") // 2
    if rows % (16 * chips) or columns % (2 * LANES):
        return [lax.all_gather(jnp.concatenate([shard, small], axis=1), "wshard", axis=0, tiled=True)]
    mine = lax.axis_index("expert")
    first = mine // 2 * (rows // chips)
    chunk = lax.dynamic_slice(shard, (first, mine % 2 * (columns // 2)), (rows // chips, columns // 2))
    beside = lax.dynamic_slice(small, (first, 0), (rows // chips, small.shape[1]))
    chunk = jnp.concatenate([chunk, beside], axis=1)
    return [chunk] + [swap(chunk, "wshard", mask) for mask in range(1, lax.axis_size("wshard"))]


def place_weight(pieces, target, small, expert_id, shard_id, shards):
    rows, columns = target.shape
    if len(pieces) == 1:
        target[...] = pieces[0][:, :columns]
        small[...] = pieces[0][:, columns:]
        return
    chips = len(pieces) // 2
    chunk = rows // shards // chips
    for mask, piece in enumerate(pieces):
        source = expert_id ^ mask
        column = pl.multiple_of(source % 2 * (columns // 2), LANES)
        for step in range(shards):
            row = (shard_id ^ step) * (rows // shards) + source // 2 * chunk
            row = pl.multiple_of(row, 16)
            lines = slice(step * chunk, (step + 1) * chunk)
            target[pl.ds(row, chunk), pl.ds(column, columns // 2)] = piece[lines, : columns // 2]
            if mask % 2 == 0:
                small[pl.ds(row, chunk), :] = piece[lines, columns // 2 :]


def place_blocks(pieces, target, expert_id, change=None):
    for mask, piece in enumerate(pieces):
        count = piece.shape[0]
        start = pl.multiple_of((expert_id ^ mask) * count, count)
        block = piece[...]
        target[pl.ds(start, count), :] = block if change is None else change(block)


def bias_rows(window, head, rows, keys):
    row = window[pl.ds(head, 1), :]
    width = row.shape[1]
    spread = jnp.broadcast_to(row, (rows, width))
    return pltpu.roll(spread, width - (rows - 1), 1, stride=1, stride_axis=0)[:, :keys]


def pair_rows(block, head_dim):
    lane = lax.broadcasted_iota(jnp.int32, block.shape, 1)
    zero = jnp.zeros_like(block)
    return jnp.concatenate(
        [jnp.where(lane < head_dim, block, zero), jnp.where(lane < head_dim, zero, block)], axis=0
    )


def pair_join(both, rows, head_dim):
    lane = lax.broadcasted_iota(jnp.int32, (rows, both.shape[1]), 1)
    return jnp.where(lane < head_dim, both[:rows], both[rows:])


def bucket_hot(window_ref, buckets):
    width = window_ref.shape[1]
    index = lax.broadcasted_iota(jnp.int32, (buckets, width), 0)
    return (index == window_ref[...]).astype(BF)


def whole(shape):
    return pl.BlockSpec(shape, lambda *_: (0,) * len(shape))


def call(body, args, outs, scratch=(), name=None, us=1.0):
    ids = pl.BlockSpec(memory_space=pltpu.SMEM)
    return pl.pallas_call(
        body,
        in_specs=[ids] + [pl.BlockSpec(memory_space=pltpu.VMEM)] * (len(args) - 1),
        out_specs=[pl.BlockSpec(memory_space=pltpu.VMEM)] * len(outs),
        out_shape=[jax.ShapeDtypeStruct(shape, kind) for shape, kind in outs],
        scratch_shapes=list(scratch),
        compiler_params=pltpu.CompilerParams(vmem_limit_bytes=VMEM_BYTES),
        cost_estimate=cost(us),
        name=name,
    )(*args)


def cost(us):
    return pl.CostEstimate(flops=int(us * 1e9), bytes_accessed=int(us * 1e6), transcendentals=0)


def normalize(block, gain):
    values = block.astype(F32)
    scale = lax.rsqrt(jnp.mean(values * values, axis=1, keepdims=True) + EPS)
    return (values * scale * gain).astype(BF)


def forward_body(sizes, *refs):
    devices, shards, heads, head_dim, buckets, experts, in_count = sizes
    refs = list(refs)
    ids = refs.pop(0)
    tokens = [refs.pop(0) for _ in range(devices)]
    in_pieces = [refs.pop(0) for _ in range(in_count)]
    window_ref, mirror_ref = [refs.pop(0) for _ in range(2)]
    xn_all, joined, joined_own, ext, w_in, window, mirror, gains, small = refs
    expert_id = ids[0]
    shard_id = ids[1]
    rows, width = tokens[0].shape
    keys = rows * devices
    place_weight(in_pieces, w_in, small, expert_id, shard_id, shards)
    turned = small[...].astype(F32).T
    gains[...] = turned[experts : experts + 8, :]
    gain_one = gains[0:1, :]
    place_blocks(tokens, xn_all, expert_id, lambda block: normalize(block, gain_one))
    head_rows = window.shape[0]
    per_shard = buckets // shards
    spot = lax.broadcasted_iota(jnp.int32, (buckets, width), 1)
    bucket = lax.broadcasted_iota(jnp.int32, (buckets, width), 0)
    spot_hot = (spot == bucket // per_shard * (width // shards) + bucket % per_shard).astype(BF)
    table = dot(turned[experts + 2 : experts + 2 + head_rows, :].astype(BF), spot_hot, NT).astype(BF)
    column_block = 2 * LANES
    row_block = min(1024, keys)

    def project(step, carry):
        row = pl.multiple_of(step // (3 * width // column_block) * row_block, row_block)
        column = pl.multiple_of(step % (3 * width // column_block) * column_block, column_block)
        joined[pl.ds(row, row_block), pl.ds(column, column_block)] = dot(
            xn_all[pl.ds(row, row_block), :], w_in[:, pl.ds(column, column_block)]
        ).astype(BF)
        return carry

    lax.fori_loop(0, (3 * width // column_block) * (keys // row_block), project, 0)
    window[...] = dot(table, bucket_hot(window_ref, buckets))
    mirror[...] = dot(table, bucket_hot(mirror_ref, buckets))
    own = pl.multiple_of(expert_id * rows, rows)
    joined_own[...] = joined[pl.ds(own, rows), :]
    lane = lax.broadcasted_iota(jnp.int32, (rows, LANES), 1)

    def attend(pair, masses):
        column = pl.multiple_of(pair * LANES, LANES)
        queries = pair_rows(joined_own[:, pl.ds(column, LANES)], head_dim)
        scores = dot(queries, joined[:, pl.ds(width + column, LANES)], NT)
        scores = scores + jnp.concatenate(
            [bias_rows(window, 2 * pair + k, rows, keys) for k in range(2)], axis=0
        )
        top = jnp.max(scores, axis=1, keepdims=True)
        probs = jnp.exp(scores - top)
        mass = jnp.sum(probs, axis=1, keepdims=True)
        mixed = dot(probs.astype(BF), joined[:, pl.ds(2 * width + column, LANES)]) / mass
        ext[:, pl.ds(column, LANES)] = pair_join(mixed, rows, head_dim).astype(BF)
        total = top + jnp.log(mass)
        masses = jnp.where(lane == 2 * pair, total[:rows], masses)
        return jnp.where(lane == 2 * pair + 1, total[rows:], masses)

    masses = lax.fori_loop(0, heads // 2, attend, jnp.zeros((rows, LANES), F32))
    high = masses.astype(BF).astype(F32)
    middle = (masses - high).astype(BF).astype(F32)
    low = (masses - high - middle).astype(BF).astype(F32)
    ext[:, width:] = (high + pltpu.roll(middle, 32, 1) + pltpu.roll(low, 64, 1)).astype(BF)


def route_body(experts, ids, w_out, tokens, ext, gains, router, chosen, slots, after, gate, send):
    rows, width = tokens.shape
    lane = lax.broadcasted_iota(jnp.int32, (rows, LANES), 1)
    post = tokens[...].astype(F32) + dot(ext[:, :width], w_out[...])
    after[...] = post
    xn_two = normalize(post, gains[1:2, :])
    logits = jnp.where(lane < experts, dot(xn_two, router[...]), -1e30)
    weights = jnp.exp(logits - jnp.max(logits, axis=1, keepdims=True))
    weights = weights / jnp.sum(weights, axis=1, keepdims=True)
    gate[...] = jnp.broadcast_to(
        jnp.sum(weights * chosen[...].astype(F32), axis=1, keepdims=True), (rows, LANES)
    )
    send[...] = dot(slots[...], xn_two).astype(BF)


def slot_pick(count, total, capacity, which):
    row = lax.broadcasted_iota(jnp.int32, (count, total), 0)
    column = lax.broadcasted_iota(jnp.int32, (count, total), 1)
    block = total // count * capacity
    return (column == row // capacity * block + which * capacity + row % capacity).astype(BF)


def upstream_body(sizes, ids, chunks, w_down, up_ref, spread_ref):
    shards, per_device, capacity = sizes
    total = chunks.shape[0] // shards
    count = total // per_device
    pick = slot_pick(count, total, capacity, pl.program_id(0))
    for step in range(shards):
        start = pl.multiple_of((ids[1] ^ step) * total, total)
        up_ref[0, step * count : (step + 1) * count, :] = dot(pick, chunks[pl.ds(start, total), :]).astype(BF)
    spread_ref[0] = dot(up_ref[0], w_down[0])


def expert_body(sizes, ids, rows_in, ups_in, spread_in, w_up, router, back_ref, x_ref, up_ref, hidden_ref, pre_ref, logit_ref):
    experts, per_device, capacity = sizes
    which = pl.program_id(0)
    mine = ids[0] * per_device + which
    total = rows_in.shape[0]
    count = total // per_device
    pick = slot_pick(count, total, capacity, which)
    x = dot(pick, rows_in[...]).astype(BF)
    lane = lax.broadcasted_iota(jnp.int32, (count, LANES), 1)
    logits = jnp.where(lane < experts, dot(x, router[...]), -1e30)
    probs = jnp.exp(logits - jnp.max(logits, axis=1, keepdims=True))
    probs = probs / jnp.sum(probs, axis=1, keepdims=True)
    hot = (lane == mine).astype(F32)
    gate = jnp.sum(probs * hot, axis=1, keepdims=True)
    pre = dot(x, w_up[0])
    inner = 0.7978845608028654 * (pre + 0.044715 * pre * pre * pre)
    bend = jnp.tanh(inner)
    hidden = 0.5 * pre * (1.0 + bend)
    slope = 0.5 * (1.0 + bend) + 0.5 * pre * (1.0 - bend * bend) * (
        0.7978845608028654 * (1.0 + 3.0 * 0.044715 * pre * pre)
    )
    hidden_low = hidden.astype(BF)
    spread = spread_in[0]
    gate_part = jnp.sum(hidden_low.astype(F32) * spread, axis=1, keepdims=True)
    pre_grad = (gate * spread * slope).astype(BF)
    logit_grad = gate_part * probs * (hot - gate)
    back = dot(pre_grad, w_up[0], NT) + dot_two(logit_grad, router[...], NT)
    x_ref[0] = x
    up_ref[0] = (gate * ups_in[0].astype(F32)).astype(BF)
    hidden_ref[0] = hidden_low
    pre_ref[0] = pre_grad
    logit_ref[0] = logit_grad
    back = dot(pick, back.astype(BF), TN).astype(BF)

    @pl.when(which == 0)
    def _():
        back_ref[...] = back

    @pl.when(which > 0)
    def _():
        back_ref[...] = (back_ref[...].astype(F32) + back.astype(F32)).astype(BF)


def expert_weights_body(sizes, ids, *refs):
    shards, per_device, capacity = sizes
    refs = list(refs)
    x, up, hidden, pre, logit = [
        jnp.concatenate([refs.pop(0)[0] for _ in range(shards)], axis=0) for _ in range(5)
    ]
    w_down, out_ref, up_grad, down_grad, router_part = refs
    which = pl.program_id(0)
    down_grad[0] = dot(up, hidden, TN)
    up_grad[0] = dot(x, pre, TN)
    router_add = dot_two(logit, x, TN)
    out = dot(hidden, w_down[0], NT).astype(BF)
    count = out.shape[0] // shards
    total = count * per_device
    pick = slot_pick(count, total, capacity, which)
    parts = [dot(pick, out[m * count : (m + 1) * count], TN).astype(BF) for m in range(shards)]
    places = [pl.ds(pl.multiple_of((ids[1] ^ m) * total, total), total) for m in range(shards)]

    @pl.when(which == 0)
    def _():
        router_part[...] = router_add
        for place, part in zip(places, parts):
            out_ref[place, :] = part

    @pl.when(which > 0)
    def _():
        router_part[...] = router_part[...] + router_add
        for place, part in zip(places, parts):
            out_ref[place, :] = (out_ref[place, :].astype(F32) + part.astype(F32)).astype(BF)


def norm_back(values, gain, grad):
    scale = lax.rsqrt(jnp.mean(values * values, axis=1, keepdims=True) + EPS)
    unit = values * scale
    inner = grad * gain
    gain_grad = jnp.sum(grad * unit, axis=0, keepdims=True)
    return scale * (inner - unit * jnp.mean(inner * unit, axis=1, keepdims=True)), gain_grad


def residual_body(ids, returned, back_slots, after, upstream, gains, resid, resid_low, gain_part):
    grad = dot(back_slots[...], returned[...])
    value, part = norm_back(after[...], gains[1:2, :], grad)
    value = value + upstream[...].astype(F32)
    resid[...] = value
    resid_low[...] = value.astype(BF)
    gain_part[...] = part


def result_body(ids, returned, back_slots, after, gate, result):
    rows = dot(back_slots[...], returned[...]).astype(BF).astype(F32)
    result[...] = (after[...] + gate[:, :1] * rows).astype(BF)


def diagonal_parts(block, width):
    rows, keys = block.shape
    total = jnp.zeros((8, width), F32)
    for group in range(rows // 8):
        part = jnp.concatenate(
            [block[group * 8 : group * 8 + 8], jnp.zeros((8, width - keys), F32)], axis=1
        )
        total = total + pltpu.roll(part, rows - 8 - 8 * group, 1)
    return total


def member_rows(head_rows, width, head_dim):
    head_of = lax.broadcasted_iota(jnp.int32, (head_rows, width), 1) // head_dim
    return (head_of == lax.broadcasted_iota(jnp.int32, (head_rows, width), 0)).astype(BF)


def part_rows(head_rows):
    part_of = lax.broadcasted_iota(jnp.int32, (head_rows, LANES), 1) % 32
    return (part_of == lax.broadcasted_iota(jnp.int32, (head_rows, LANES), 0)).astype(BF)


def query_body(sizes, ids, resid_low, ext, joined_own, w_out, window, window_ref, keys_in, values_in, query_grad, table_part, grads, delta, mass, diagonals):
    head_dim, buckets = sizes
    pair = pl.program_id(0)
    rows, width = resid_low.shape
    keys = keys_in.shape[0]
    head_rows, span = window.shape

    @pl.when(pair == 0)
    def _():
        low = dot(resid_low[...], w_out[...], NT).astype(BF)
        grads[...] = low
        product = low.astype(F32) * ext[:, :width].astype(F32)
        delta[...] = dot_two(product, member_rows(head_rows, width, head_dim), NT)
        mass[...] = dot(ext[:, width:], part_rows(head_rows), NT)

    head_lane = lax.broadcasted_iota(jnp.int32, (rows, head_rows), 1)

    def column_of(ref):
        return jnp.concatenate(
            [
                jnp.sum(jnp.where(head_lane == 2 * pair + k, ref[...], 0.0), axis=1, keepdims=True)
                for k in range(2)
            ],
            axis=0,
        )

    column = pl.multiple_of(pair * LANES, LANES)
    queries = pair_rows(joined_own[:, pl.ds(column, LANES)], head_dim)
    grad_own = pair_rows(grads[:, pl.ds(column, LANES)], head_dim)
    scores = dot(queries, keys_in[...], NT) + jnp.concatenate(
        [bias_rows(window, 2 * pair + k, rows, keys) for k in range(2)], axis=0
    )
    probs = jnp.exp(scores - column_of(mass))
    score_grad = (probs * (dot(grad_own, values_in[...], NT) - column_of(delta))).astype(BF)
    query_grad[0] = pair_join(dot(score_grad, keys_in[...]), rows, head_dim).astype(BF)
    wide = score_grad.astype(F32)
    for k in range(2):
        start = pl.multiple_of((2 * pair + k) * 8, 8)
        diagonals[pl.ds(start, 8), :] = diagonal_parts(wide[k * rows : (k + 1) * rows], span)

    @pl.when(pair == pl.num_programs(0) - 1)
    def _():
        every = diagonals[...]
        total_rows = every.shape[0]
        lined = jnp.zeros((total_rows, span), F32)
        place = lax.broadcasted_iota(jnp.int32, (total_rows, span), 0) % 8
        for step in range(8):
            moved = every if step == 7 else pltpu.roll(every, 7 - step, 1)
            lined = jnp.where(place == step, moved, lined)
        line_rows = lax.broadcasted_iota(jnp.int32, (head_rows, total_rows), 1) // 8
        fold = (line_rows == lax.broadcasted_iota(jnp.int32, (head_rows, total_rows), 0)).astype(BF)
        high = lined.astype(BF)
        low = (lined - high.astype(F32)).astype(BF)
        sums = dot(fold, high) + dot(fold, low)
        table_part[...] = dot_two(sums, bucket_hot(window_ref, buckets), NT)


def key_body(sizes, *refs):
    devices, heads, head_dim = sizes
    refs = list(refs)
    ids = refs.pop(0)
    resid_pieces = [refs.pop(0) for _ in range(devices)]
    ext_all, joined_own, w_out, mirror, query_grad, queries_in = [refs.pop(0) for _ in range(6)]
    blocks, grads, delta_rows, mass_rows = refs
    expert_id = ids[0]
    pair = pl.program_id(0)
    rows, width = resid_pieces[0].shape
    keys = rows * devices
    head_rows = mirror.shape[0]
    pairs = heads // 2

    @pl.when(pair == 0)
    def _():
        place_blocks(resid_pieces, grads, expert_id)
        mass_rows[...] = dot(part_rows(head_rows), ext_all[:, width:], NT)
        member = member_rows(head_rows, width, head_dim)
        step = min(1024, keys)
        for start in range(0, keys, step):
            low = dot(grads[start : start + step, :], w_out[...], NT).astype(BF)
            grads[start : start + step, :] = low
            product = low.astype(F32) * ext_all[start : start + step, :width].astype(F32)
            high = product.astype(BF)
            rest = (product - high.astype(F32)).astype(BF)
            delta_rows[:, start : start + step] = dot(member, high, NT) + dot(member, rest, NT)
        blocks[:pairs] = query_grad[...]
        for block in range(pairs):
            blocks[3 * pairs + block] = resid_pieces[0][:, block * LANES : (block + 1) * LANES]
        for block in range(4 * pairs, blocks.shape[0]):
            blocks[block] = jnp.zeros((rows, LANES), BF)

    def row_of(ref):
        return jnp.concatenate(
            [jnp.broadcast_to(ref[pl.ds(2 * pair + k, 1), :], (rows, keys)) for k in range(2)],
            axis=0,
        )

    column = pl.multiple_of(pair * LANES, LANES)
    grad_all = grads[:, pl.ds(column, LANES)]
    key_own = pair_rows(joined_own[:, pl.ds(width + column, LANES)], head_dim)
    value_own = pair_rows(joined_own[:, pl.ds(2 * width + column, LANES)], head_dim)
    scores = dot(key_own, queries_in[...], NT) + jnp.concatenate(
        [bias_rows(mirror, 2 * pair + k, rows, keys) for k in range(2)], axis=0
    )
    probs = jnp.exp(scores - row_of(mass_rows))
    score_grad = (probs * (dot(value_own, grad_all, NT) - row_of(delta_rows))).astype(BF)
    blocks[pairs + pair] = pair_join(dot(score_grad, queries_in[...]), rows, head_dim).astype(BF)
    blocks[2 * pairs + pair] = pair_join(dot(probs.astype(BF), grad_all), rows, head_dim).astype(BF)


def source_body(ids, blocks, w_in, tokens, gains, resid, tokens_grad, gain_part, joined):
    for block in range(joined.shape[1] // LANES):
        joined[:, block * LANES : (block + 1) * LANES] = blocks[block]
    grad = dot(joined[...], w_in[...], NT)
    value, part = norm_back(tokens[...].astype(F32), gains[0:1, :], grad)
    tokens_grad[...] = (value + resid[...]).astype(BF)
    gain_part[...] = part


def weight_body(sizes, ids, xn_all, ext_all, received, lines, part, columns):
    per, pairs, shards = sizes
    devices, _, rows, _ = received.shape
    width = xn_all.shape[1]
    rows_each = width // shards
    for source in range(devices):
        for block in range(per):
            columns[source * rows : (source + 1) * rows, block * LANES : (block + 1) * LANES] = received[
                source, block
            ]

    def store(value, line):
        for owner in range(shards):
            part[owner, :rows_each, line] = value[owner * rows_each : (owner + 1) * rows_each].astype(BF)

    step = per if 3 * pairs % per == 0 else 1
    for block in range(0, per, step):
        inside = ids[0] * per + block < 3 * pairs
        line = slice(block * LANES, (block + step) * LANES)

        @pl.when(inside)
        def _():
            store(dot(xn_all[...], columns[:, line], TN), line)

        @pl.when(jnp.logical_not(inside))
        def _():
            store(dot(ext_all[:, :width], columns[:, line], TN), line)

    part[:, rows_each:, :] = lines[...]


def spread_body(sizes, ids, *refs):
    per, pairs = sizes
    pieces, (in_grad, out_grad, lines) = refs[:-3], refs[-3:]
    rows = in_grad.shape[0]
    total = None
    for mask, piece in enumerate(pieces):
        source = ids[0] ^ mask
        extra = piece[rows:, :].astype(F32)
        total = extra if total is None else total + extra
        for block in range(per):
            index = source * per + block
            values = piece[:rows, block * LANES : (block + 1) * LANES].astype(F32)

            @pl.when(index < 3 * pairs)
            def _():
                in_grad[:, pl.ds(pl.multiple_of(index * LANES, LANES), LANES)] = values

            @pl.when(jnp.logical_and(index >= 3 * pairs, index < 4 * pairs))
            def _():
                out_grad[:, pl.ds(pl.multiple_of((index - 3 * pairs) * LANES, LANES), LANES)] = values

    lines[...] = total


def pad_to(x, shape):
    return jnp.pad(x, [(0, size - have) for size, have in zip(shape, x.shape)])


def local(
    tokens, gain_attn, gain_mix, attn_in, attn_out, router, bias_table, expert_in, expert_down, routes, buckets, out_grad
):
    own_tokens = tokens[0]
    own_grad = out_grad[0]
    rows, width = own_tokens.shape
    devices = lax.axis_size("expert")
    shards = lax.axis_size("wshard")
    expert_id = lax.axis_index("expert")
    shard_id = lax.axis_index("wshard")
    heads = bias_table.shape[1]
    head_dim = width // heads
    experts = router.shape[1]
    bucket_count = bias_table.shape[0] * shards
    per_device = expert_in.shape[0]
    keys = rows * devices
    capacity = 3 * rows // (2 * experts)
    part = width // shards
    ids = jnp.stack([expert_id, shard_id]).astype(jnp.int32)

    table_rows = bias_table.shape[0]
    head_rows = 16
    small = jnp.concatenate(
        [
            router,
            gain_attn[:, None],
            gain_mix[:, None],
            pad_to(bias_table, (part, LANES - experts - 2)),
        ],
        axis=1,
    )
    in_chunks = weight_chunks(attn_in, small)
    chip_tokens = chip_pieces(own_tokens)
    window_width = keys + rows
    start = keys - 1 - expert_id * rows - (rows - 1)
    window_buckets = lax.dynamic_slice(jnp.pad(buckets, (0, rows)), (start,), (window_width,))
    mirror_buckets = lax.dynamic_slice(jnp.pad(buckets[::-1], (0, rows)), (start,), (window_width,))
    last = jnp.arange(window_width) == window_width - 1
    window_buckets = jnp.where(last, -1, window_buckets)[None]
    mirror_buckets = jnp.where(last, -1, mirror_buckets)[None]

    route = routes[0]
    earlier = jnp.arange(rows)[None, :] < jnp.arange(rows)[:, None]
    rank = jnp.sum(((route[None, :] == route[:, None]) & earlier).astype(jnp.int32), axis=1)
    slot = route * capacity + rank
    slot_count = experts * capacity
    slots = (jnp.arange(slot_count)[:, None] == slot[None, :]).astype(BF)
    back_slots = (slot[:, None] == jnp.arange(slot_count)[None, :]).astype(BF)
    chosen = (route[:, None] == jnp.arange(LANES)[None, :]).astype(BF)

    block = per_device * capacity

    def scatter_rows(parts):
        mine = lax.dynamic_index_in_dim(parts, shard_id, 0, keepdims=False).astype(F32)
        for mask in range(1, shards):
            sent = lax.dynamic_index_in_dim(parts, shard_id ^ mask, 0, keepdims=False)
            mine = mine + swap(sent, "wshard", mask).astype(F32)
        return mine

    def exchange(slot_rows):
        blocks = slot_rows.reshape(devices, block, width)
        moved = lax.all_to_all(blocks, "expert", split_axis=0, concat_axis=0, tiled=True)
        return moved.reshape(devices * block, width)

    def sum_back(parts):
        total = parts[0].astype(F32)
        for mask in range(1, shards):
            total = total + swap(parts[mask], "wshard", mask).astype(F32)
        return total.astype(BF)

    chip_tokens, in_chunks, attn_out, ups = tie(
        chip_tokens, in_chunks, attn_out, dot(slots, own_grad).astype(BF)
    )
    in_pieces = in_chunks
    if len(in_chunks) > 1:
        in_pieces = chip_pieces(jnp.concatenate(in_chunks, axis=0))
    token_pieces = core_pieces(chip_tokens)
    w_out = lax.all_gather(attn_out, "wshard", axis=0, tiled=True)
    in_pieces, token_pieces, ups = tie(in_pieces, token_pieces, exchange(ups))
    if len(in_pieces) > 1:
        in_pieces = core_pieces(in_pieces)
    ups_all = lax.all_gather(ups, "wshard", axis=0, tiled=True)

    sizes = (devices, shards, heads, head_dim, bucket_count, experts, len(in_pieces))
    xn_all, joined, joined_own, ext, w_in, window, mirror, gains, router_pad = call(
        functools.partial(forward_body, sizes),
        [ids, *token_pieces, *in_pieces, window_buckets, mirror_buckets],
        [
            ((keys, width), BF),
            ((keys, 3 * width), BF),
            ((rows, 3 * width), BF),
            ((rows, width + LANES), BF),
            ((width, 3 * width), BF),
            ((head_rows, window_width), F32),
            ((head_rows, window_width), F32),
            ((8, width), F32),
            ((width, LANES), BF),
        ],
        name="attention_forward",
        us=0.2,
    )
    after, gate, send = call(
        functools.partial(route_body, experts),
        [ids, w_out, own_tokens, ext, gains, router_pad, chosen, slots],
        [((rows, width), F32), ((rows, LANES), F32), ((slot_count, width), BF)],
        name="route",
        us=0.2,
    )
    rows_own = exchange(send)
    total = devices * block
    count = total // per_device
    ff = expert_in.shape[2]
    by_expert = pl.BlockSpec((1, width, ff), lambda k: (k, 0, 0))
    kept_ff = pl.BlockSpec((1, count, ff), lambda k: (k, 0, 0))
    kept_width = pl.BlockSpec((1, count, width), lambda k: (k, 0, 0))
    kept_lanes = pl.BlockSpec((1, count, LANES), lambda k: (k, 0, 0))
    upstream_width = pl.BlockSpec((1, shards * count, width), lambda k: (k, 0, 0))
    upstream_ff = pl.BlockSpec((1, shards * count, ff), lambda k: (k, 0, 0))
    ups_all, spread_all = pl.pallas_call(
        functools.partial(upstream_body, (shards, per_device, capacity)),
        grid=(per_device,),
        in_specs=[pl.BlockSpec(memory_space=pltpu.SMEM), whole((shards * total, width)), by_expert],
        out_specs=[upstream_width, upstream_ff],
        out_shape=[
            jax.ShapeDtypeStruct((per_device, shards * count, width), BF),
            jax.ShapeDtypeStruct((per_device, shards * count, ff), F32),
        ],
        compiler_params=pltpu.CompilerParams(vmem_limit_bytes=VMEM_BYTES),
        cost_estimate=cost(5.0),
        name="upstream",
    )(ids, ups_all, expert_down)
    rows_own, ups_all, spread_all = tie(rows_own, ups_all, spread_all)
    row_chunks = {0: rows_own}
    steps = [1 << bit for bit in reversed(range((shards - 1).bit_length()))]
    row_chunks.update({step: swap(rows_own, "wshard", step) for step in steps})
    ext_later, _ = tie(ext, rows_own)
    ext_all = lax.all_gather(ext_later, "expert", axis=0, tiled=True)
    kept = [[], [], [], [], []]
    back_parts = []
    for step in range(shards):
        row_chunk = row_chunks[step]
        if step:
            row_chunk, _ = tie(row_chunk, back_parts[-1])
        back, *saved = pl.pallas_call(
            functools.partial(expert_body, (experts, per_device, capacity)),
            grid=(per_device,),
            in_specs=[
                pl.BlockSpec(memory_space=pltpu.SMEM),
                whole((total, width)),
                pl.BlockSpec((1, count, width), lambda k, step=step: (k, step, 0)),
                pl.BlockSpec((1, count, ff), lambda k, step=step: (k, step, 0)),
                by_expert,
                whole((width, LANES)),
            ],
            out_specs=[whole((total, width)), kept_width, kept_width, kept_ff, kept_ff, kept_lanes],
            out_shape=[
                jax.ShapeDtypeStruct((total, width), BF),
                jax.ShapeDtypeStruct((per_device, count, width), BF),
                jax.ShapeDtypeStruct((per_device, count, width), BF),
                jax.ShapeDtypeStruct((per_device, count, ff), BF),
                jax.ShapeDtypeStruct((per_device, count, ff), BF),
                jax.ShapeDtypeStruct((per_device, count, LANES), F32),
            ],
            compiler_params=pltpu.CompilerParams(vmem_limit_bytes=VMEM_BYTES),
            cost_estimate=cost(0.5),
            name="experts",
        )(ids, row_chunk, ups_all, spread_all, expert_in, router_pad)
        back_parts.append(back)
        for group, value in zip(kept, saved):
            group.append(value)
        if step == 1:
            for mask in range(1, shards):
                nearer = mask & (-mask)
                if mask != nearer:
                    value, _ = tie(row_chunks[mask ^ nearer], back)
                    row_chunks[mask] = swap(value, "wshard", nearer)
    kept, back_sum = tie(kept, sum_back(back_parts))
    returned_grad = exchange(back_sum)
    out_parts, up_grad, down_grad, router_part = pl.pallas_call(
        functools.partial(expert_weights_body, (shards, per_device, capacity)),
        grid=(per_device,),
        in_specs=[pl.BlockSpec(memory_space=pltpu.SMEM)]
        + [kept_width] * (2 * shards)
        + [kept_ff] * (2 * shards)
        + [kept_lanes] * shards
        + [by_expert],
        out_specs=[whole((shards * total, width)), by_expert, by_expert, whole((LANES, width))],
        out_shape=[
            jax.ShapeDtypeStruct((shards * total, width), BF),
            jax.ShapeDtypeStruct((per_device, width, ff), F32),
            jax.ShapeDtypeStruct((per_device, width, ff), F32),
            jax.ShapeDtypeStruct((LANES, width), F32),
        ],
        compiler_params=pltpu.CompilerParams(vmem_limit_bytes=VMEM_BYTES),
        cost_estimate=cost(8.0),
        name="expert_weights",
    )(ids, *[value for group in kept for value in group], expert_down)
    out_parts, router_part, returned_grad = tie(out_parts, router_part, returned_grad)
    resid, resid_low, gain_two_part = call(
        residual_body,
        [ids, returned_grad, back_slots, after, own_grad, gains],
        [((rows, width), F32), ((rows, width), BF), ((1, width), F32)],
        name="residual",
        us=2.0,
    )
    out_parts, _ = tie(out_parts, resid_low)
    out_sum = lax.psum_scatter(out_parts, "wshard", scatter_dimension=0, tiled=True)
    resid_pieces = chip_pieces(resid_low)
    pairs = heads // 2

    def column_block(offset):
        return pl.BlockSpec((keys, LANES), lambda p: (0, offset * pairs + p))

    query_grad, table_part = pl.pallas_call(
        functools.partial(query_body, (head_dim, bucket_count)),
        grid=(pairs,),
        in_specs=[
            pl.BlockSpec(memory_space=pltpu.SMEM),
            whole((rows, width)),
            whole((rows, width + LANES)),
            whole((rows, 3 * width)),
            whole((width, width)),
            whole((head_rows, window_width)),
            whole((1, window_width)),
            column_block(1),
            column_block(2),
        ],
        out_specs=[pl.BlockSpec((1, rows, LANES), lambda p: (p, 0, 0)), whole((head_rows, bucket_count))],
        out_shape=[
            jax.ShapeDtypeStruct((pairs, rows, LANES), BF),
            jax.ShapeDtypeStruct((head_rows, bucket_count), F32),
        ],
        scratch_shapes=[
            pltpu.VMEM((rows, width), BF),
            pltpu.VMEM((rows, head_rows), F32),
            pltpu.VMEM((rows, head_rows), F32),
            pltpu.VMEM((head_rows * 8, window_width), F32),
        ],
        compiler_params=pltpu.CompilerParams(vmem_limit_bytes=VMEM_BYTES),
        cost_estimate=cost(10.0),
        name="query_grad",
    )(ids, resid_low, ext, joined_own, w_out, window, window_buckets, joined, joined)
    per = -(-4 * pairs // devices)
    resid_pieces, query_grad = tie(resid_pieces, query_grad)
    resid_pieces = core_pieces(resid_pieces)
    (blocks,) = pl.pallas_call(
        functools.partial(key_body, (devices, heads, head_dim)),
        grid=(pairs,),
        in_specs=[pl.BlockSpec(memory_space=pltpu.SMEM)]
        + [whole((rows, width))] * devices
        + [
            whole((keys, width + LANES)),
            whole((rows, 3 * width)),
            whole((width, width)),
            whole((head_rows, window_width)),
            whole((pairs, rows, LANES)),
            column_block(0),
        ],
        out_specs=[whole((per * devices, rows, LANES))],
        out_shape=[
            jax.ShapeDtypeStruct((per * devices, rows, LANES), BF),
        ],
        scratch_shapes=[
            pltpu.VMEM((keys, width), BF),
            pltpu.VMEM((head_rows, keys), F32),
            pltpu.VMEM((head_rows, keys), F32),
        ],
        compiler_params=pltpu.CompilerParams(vmem_limit_bytes=VMEM_BYTES),
        cost_estimate=cost(12.0),
        name="key_grad",
    )(ids, *resid_pieces, ext_all, joined_own, w_out, mirror, query_grad, joined)
    blocks, out_sum = tie(blocks, out_sum)
    received = lax.all_to_all(
        blocks.reshape(devices, per, rows, LANES), "expert", split_axis=0, concat_axis=0, tiled=True
    )
    tokens_grad, gain_one_part = call(
        source_body,
        [ids, blocks, w_in, own_tokens, gains, resid],
        [((rows, width), BF), ((1, width), F32)],
        [pltpu.VMEM((rows, 3 * width), BF)],
        name="source_grad",
        us=4.0,
    )
    table_line = table_part[:heads].T.reshape(shards, table_rows * heads)
    table_line = pad_to(table_line, (shards, part)).reshape(1, width)
    lines = jnp.concatenate([router_part[:experts], gain_one_part, gain_two_part, table_line], axis=0)
    line_count = lines.shape[0]
    groups = per * LANES // part
    line_rows = -(-line_count // (16 * groups)) * 16
    lines = pad_to(lines, (groups * line_rows, width)).reshape(groups, line_rows, shards, part)
    lines = lines.transpose(2, 1, 0, 3).reshape(shards, line_rows, groups * part)
    lines = pad_to(lines, (shards, line_rows, per * LANES)).astype(BF)
    (weight_part,) = call(
        functools.partial(weight_body, (per, pairs, shards)),
        [ids, xn_all, ext_all, received, lines],
        [((shards, part + line_rows, per * LANES), BF)],
        [pltpu.VMEM((keys, per * LANES), BF)],
        name="weight_grads",
        us=4.0,
    )
    weight_part, out_sum = tie(weight_part, out_sum)
    mine = scatter_rows(weight_part).astype(BF)
    returned_rows = exchange(out_sum)
    mine, returned_rows = tie(mine, returned_rows)
    pieces = chip_pieces(mine)
    (result,) = call(
        result_body,
        [ids, returned_rows, back_slots, after, gate],
        [((rows, width), BF)],
        name="result",
        us=2.0,
    )
    pieces, result = tie(pieces, result)
    attn_in_grad, attn_out_grad, lines = call(
        functools.partial(spread_body, (per, pairs)),
        [ids, *core_pieces(pieces)],
        [((part, 3 * width), F32), ((part, width), F32), ((line_rows, per * LANES), F32)],
        name="spread",
        us=2.0,
    )
    lines = lines[:, : groups * part].reshape(line_rows, groups, part).transpose(1, 0, 2)
    lines = lines.reshape(groups * line_rows, part)
    router_grad = lines[:experts].T
    table_grad = lines[experts + 2, : table_rows * heads].reshape(table_rows, heads)
    return (
        result[None],
        tokens_grad[None],
        lines[experts],
        lines[experts + 1],
        attn_in_grad,
        attn_out_grad,
        router_grad,
        table_grad,
        up_grad,
        down_grad,
    )


def solution(mesh):
    return jax.shard_map(
        local,
        mesh=mesh,
        in_specs=(
            P("wshard", "expert", None),
            P("wshard"),
            P("wshard"),
            P("wshard", None),
            P("wshard", None),
            P("wshard", None),
            P("wshard", None),
            P("expert", None, "wshard"),
            P("expert", None, "wshard"),
            P("wshard", "expert"),
            P(),
            P("wshard", "expert", None),
        ),
        out_specs=(
            P("wshard", "expert", None),
            P("wshard", "expert", None),
            P("wshard"),
            P("wshard"),
            P("wshard", None),
            P("wshard", None),
            P("wshard", None),
            P("wshard", None),
            P("expert", None, "wshard"),
            P("expert", None, "wshard"),
        ),
        check_vma=False,
    )
```

```python
import functools

import jax
import jax.numpy as jnp
from jax import lax
from jax.experimental import pallas as pl
from jax.experimental.pallas import tpu as pltpu
from jax.sharding import PartitionSpec as P

BF = jnp.bfloat16
F32 = jnp.float32
EPS = 1e-06
LANES = 128
VMEM_BYTES = 60 * 1024 * 1024
NN = (((1,), (0,)), ((), ()))
NT = (((1,), (1,)), ((), ()))
TN = (((0,), (0,)), ((), ()))


def dot(a, b, dims=NN):
    return lax.dot_general(a, b, dims, preferred_element_type=F32)


def dot_two(a, b, dims=NN):
    high = a.astype(BF)
    low = (a - high.astype(F32)).astype(BF)
    return dot(high, b, dims) + dot(low, b, dims)


def swap(x, axis, mask):
    count = lax.axis_size(axis)
    return lax.ppermute(x, axis, [(i, i ^ mask) for i in range(count)])


def tie(*groups):
    return lax.optimization_barrier(groups)


def chip_pieces(x):
    return [x] + [swap(x, "expert", mask) for mask in range(2, lax.axis_size("expert"), 2)]


def core_pieces(pieces):
    return [block for piece in pieces for block in (piece, swap(piece, "expert", 1))]


def weight_chunks(shard, small):
    rows, columns = shard.shape
    chips = lax.axis_size("expert") // 2
    if rows % (16 * chips) or columns % (2 * LANES):
        return [lax.all_gather(jnp.concatenate([shard, small], axis=1), "wshard", axis=0, tiled=True)]
    mine = lax.axis_index("expert")
    first = mine // 2 * (rows // chips)
    chunk = lax.dynamic_slice(shard, (first, mine % 2 * (columns // 2)), (rows // chips, columns // 2))
    beside = lax.dynamic_slice(small, (first, 0), (rows // chips, small.shape[1]))
    chunk = jnp.concatenate([chunk, beside], axis=1)
    return [chunk] + [swap(chunk, "wshard", mask) for mask in range(1, lax.axis_size("wshard"))]


def doubling_steps(count):
    return [1 << bit for bit in reversed(range((count - 1).bit_length()))]


def doubling_order(count):
    order = [0]
    for step in doubling_steps(count):
        order = order + [mask ^ step for mask in order]
    return order


def place_order(gathered, target, shard_id, shards):
    rows = target.shape[0] // shards
    for index, mask in enumerate(doubling_order(shards)):
        row = pl.multiple_of((shard_id ^ mask) * rows, 16)
        target[pl.ds(row, rows), :] = gathered[index * rows : (index + 1) * rows, :]


def place_weight(pieces, target, small, expert_id, shard_id, shards):
    rows, columns = target.shape
    if len(pieces) == 1:
        target[...] = pieces[0][:, :columns]
        small[...] = pieces[0][:, columns:]
        return
    chips = len(pieces) // 2
    chunk = rows // shards // chips
    for mask, piece in enumerate(pieces):
        source = expert_id ^ mask
        column = pl.multiple_of(source % 2 * (columns // 2), LANES)
        for step in range(shards):
            row = (shard_id ^ step) * (rows // shards) + source // 2 * chunk
            row = pl.multiple_of(row, 16)
            lines = slice(step * chunk, (step + 1) * chunk)
            target[pl.ds(row, chunk), pl.ds(column, columns // 2)] = piece[lines, : columns // 2]
            if mask % 2 == 0:
                small[pl.ds(row, chunk), :] = piece[lines, columns // 2 :]


def place_blocks(pieces, target, expert_id, change=None):
    for mask, piece in enumerate(pieces):
        count = piece.shape[0]
        start = pl.multiple_of((expert_id ^ mask) * count, count)
        block = piece[...]
        target[pl.ds(start, count), :] = block if change is None else change(block)


def bias_rows(window, head, rows, keys):
    row = window[pl.ds(head, 1), :]
    width = row.shape[1]
    spread = jnp.broadcast_to(row, (rows, width))
    return pltpu.roll(spread, width - (rows - 1), 1, stride=1, stride_axis=0)[:, :keys]


def pair_rows(block, head_dim):
    lane = lax.broadcasted_iota(jnp.int32, block.shape, 1)
    zero = jnp.zeros_like(block)
    return jnp.concatenate(
        [jnp.where(lane < head_dim, block, zero), jnp.where(lane < head_dim, zero, block)], axis=0
    )


def pair_join(both, rows, head_dim):
    lane = lax.broadcasted_iota(jnp.int32, (rows, both.shape[1]), 1)
    return jnp.where(lane < head_dim, both[:rows], both[rows:])


def bucket_hot(window_ref, buckets):
    width = window_ref.shape[1]
    index = lax.broadcasted_iota(jnp.int32, (buckets, width), 0)
    return (index == window_ref[...]).astype(BF)


def whole(shape):
    return pl.BlockSpec(shape, lambda *_: (0,) * len(shape))


def call(body, args, outs, scratch=(), name=None, us=1.0, far=()):
    ids = pl.BlockSpec(memory_space=pltpu.SMEM)
    near = pl.BlockSpec(memory_space=pltpu.VMEM)
    return pl.pallas_call(
        body,
        in_specs=[ids] + [near] * (len(args) - 1),
        out_specs=[pl.BlockSpec(memory_space=pl.ANY) if k in far else near for k in range(len(outs))],
        out_shape=[jax.ShapeDtypeStruct(shape, kind) for shape, kind in outs],
        scratch_shapes=list(scratch),
        compiler_params=pltpu.CompilerParams(vmem_limit_bytes=VMEM_BYTES),
        cost_estimate=cost(us),
        name=name,
    )(*args)


def cost(us):
    return pl.CostEstimate(flops=int(us * 1e9), bytes_accessed=int(us * 1e6), transcendentals=0)


def normalize(block, gain):
    values = block.astype(F32)
    scale = lax.rsqrt(jnp.mean(values * values, axis=1, keepdims=True) + EPS)
    return (values * scale * gain).astype(BF)


def forward_body(sizes, *refs):
    devices, shards, heads, head_dim, buckets, experts, in_count = sizes
    refs = list(refs)
    ids = refs.pop(0)
    tokens = [refs.pop(0) for _ in range(devices)]
    in_pieces = [refs.pop(0) for _ in range(in_count)]
    window_ref, mirror_ref = [refs.pop(0) for _ in range(2)]
    xn_far, joined_far, joined_own, ext, window, mirror, gains, small, xn_all, joined, w_in, sems = refs
    expert_id = ids[0]
    shard_id = ids[1]
    rows, width = tokens[0].shape
    keys = rows * devices
    place_weight(in_pieces, w_in, small, expert_id, shard_id, shards)
    turned = small[...].astype(F32).T
    gains[...] = turned[experts : experts + 8, :]
    gain_one = gains[0:1, :]
    place_blocks(tokens, xn_all, expert_id, lambda block: normalize(block, gain_one))
    xn_copy = pltpu.make_async_copy(xn_all, xn_far, sems.at[0])
    xn_copy.start()
    head_rows = window.shape[0]
    per_shard = buckets // shards
    spot = lax.broadcasted_iota(jnp.int32, (buckets, width), 1)
    bucket = lax.broadcasted_iota(jnp.int32, (buckets, width), 0)
    spot_hot = (spot == bucket // per_shard * (width // shards) + bucket % per_shard).astype(BF)
    table = dot(turned[experts + 2 : experts + 2 + head_rows, :].astype(BF), spot_hot, NT).astype(BF)
    column_block = 2 * LANES
    row_block = min(1024, keys)

    def project(step, carry):
        row = pl.multiple_of(step // (3 * width // column_block) * row_block, row_block)
        column = pl.multiple_of(step % (3 * width // column_block) * column_block, column_block)
        joined[pl.ds(row, row_block), pl.ds(column, column_block)] = dot(
            xn_all[pl.ds(row, row_block), :], w_in[:, pl.ds(column, column_block)]
        ).astype(BF)
        return carry

    lax.fori_loop(0, (3 * width // column_block) * (keys // row_block), project, 0)
    joined_copy = pltpu.make_async_copy(joined, joined_far, sems.at[1])
    joined_copy.start()
    window[...] = dot(table, bucket_hot(window_ref, buckets))
    mirror[...] = dot(table, bucket_hot(mirror_ref, buckets))
    own = pl.multiple_of(expert_id * rows, rows)
    joined_own[...] = joined[pl.ds(own, rows), :]
    lane = lax.broadcasted_iota(jnp.int32, (rows, LANES), 1)

    def attend(pair, masses):
        column = pl.multiple_of(pair * LANES, LANES)
        queries = pair_rows(joined_own[:, pl.ds(column, LANES)], head_dim)
        scores = dot(queries, joined[:, pl.ds(width + column, LANES)], NT)
        scores = scores + jnp.concatenate(
            [bias_rows(window, 2 * pair + k, rows, keys) for k in range(2)], axis=0
        )
        top = jnp.max(scores, axis=1, keepdims=True)
        probs = jnp.exp(scores - top)
        mass = jnp.sum(probs, axis=1, keepdims=True)
        mixed = dot(probs.astype(BF), joined[:, pl.ds(2 * width + column, LANES)]) / mass
        ext[:, pl.ds(column, LANES)] = pair_join(mixed, rows, head_dim).astype(BF)
        total = top + jnp.log(mass)
        masses = jnp.where(lane == 2 * pair, total[:rows], masses)
        return jnp.where(lane == 2 * pair + 1, total[rows:], masses)

    masses = lax.fori_loop(0, heads // 2, attend, jnp.zeros((rows, LANES), F32))
    ext[:, width:] = spread_parts(masses)
    xn_copy.wait()
    joined_copy.wait()


def route_body(sizes, ids, w_rows, tokens, ext, gains, router, chosen, slots, after, gate, send, w_out):
    experts, shards = sizes
    rows, width = tokens.shape
    place_order(w_rows, w_out, ids[1], shards)
    lane = lax.broadcasted_iota(jnp.int32, (rows, LANES), 1)
    post = tokens[...].astype(F32) + dot(ext[:, :width], w_out[...])
    after[...] = post
    xn_two = normalize(post, gains[1:2, :])
    logits = jnp.where(lane < experts, dot(xn_two, router[...]), -1e30)
    weights = jnp.exp(logits - jnp.max(logits, axis=1, keepdims=True))
    weights = weights / jnp.sum(weights, axis=1, keepdims=True)
    gate[...] = jnp.broadcast_to(
        jnp.sum(weights * chosen[...].astype(F32), axis=1, keepdims=True), (rows, LANES)
    )
    send[...] = dot(slots[...], xn_two).astype(BF)


def slot_pick(count, total, capacity, which):
    row = lax.broadcasted_iota(jnp.int32, (count, total), 0)
    column = lax.broadcasted_iota(jnp.int32, (count, total), 1)
    block = total // count * capacity
    return (column == row // capacity * block + which * capacity + row % capacity).astype(BF)


def upstream_body(sizes, chunks, w_down, up_ref, spread_ref):
    shards, per_device, capacity = sizes
    total = chunks.shape[0] // shards
    count = total // per_device
    pick = slot_pick(count, total, capacity, pl.program_id(0))
    for index, mask in enumerate(doubling_order(shards)):
        chunk = chunks[index * total : (index + 1) * total, :]
        up_ref[0, mask * count : (mask + 1) * count, :] = dot(pick, chunk).astype(BF)
    spread_ref[0] = dot(up_ref[0], w_down[0])


def expert_body(sizes, ids, rows_in, ups_in, spread_in, w_up, router, back_ref, x_ref, up_ref, hidden_ref, pre_ref, logit_ref):
    experts, per_device, capacity = sizes
    which = pl.program_id(0)
    mine = ids[0] * per_device + which
    total = rows_in.shape[0]
    count = total // per_device
    pick = slot_pick(count, total, capacity, which)
    x = dot(pick, rows_in[...]).astype(BF)
    lane = lax.broadcasted_iota(jnp.int32, (count, LANES), 1)
    logits = jnp.where(lane < experts, dot(x, router[...]), -1e30)
    probs = jnp.exp(logits - jnp.max(logits, axis=1, keepdims=True))
    probs = probs / jnp.sum(probs, axis=1, keepdims=True)
    hot = (lane == mine).astype(F32)
    gate = jnp.sum(probs * hot, axis=1, keepdims=True)
    pre = dot(x, w_up[0])
    inner = 0.7978845608028654 * (pre + 0.044715 * pre * pre * pre)
    bend = jnp.tanh(inner)
    hidden = 0.5 * pre * (1.0 + bend)
    slope = 0.5 * (1.0 + bend) + 0.5 * pre * (1.0 - bend * bend) * (
        0.7978845608028654 * (1.0 + 3.0 * 0.044715 * pre * pre)
    )
    hidden_low = hidden.astype(BF)
    spread = spread_in[0]
    gate_part = jnp.sum(hidden_low.astype(F32) * spread, axis=1, keepdims=True)
    pre_grad = (gate * spread * slope).astype(BF)
    logit_grad = gate_part * probs * (hot - gate)
    back = dot(pre_grad, w_up[0], NT) + dot_two(logit_grad, router[...], NT)
    x_ref[0] = x
    up_ref[0] = (gate * ups_in[0].astype(F32)).astype(BF)
    hidden_ref[0] = hidden_low
    pre_ref[0] = pre_grad
    logit_ref[0] = logit_grad
    back = dot(pick, back.astype(BF), TN).astype(BF)

    @pl.when(which == 0)
    def _():
        back_ref[...] = back

    @pl.when(which > 0)
    def _():
        back_ref[...] = (back_ref[...].astype(F32) + back.astype(F32)).astype(BF)


def expert_out_body(sizes, *refs):
    shards, per_device, capacity = sizes
    refs = list(refs)
    x, hidden, logit = [
        jnp.concatenate([refs.pop(0)[0] for _ in range(shards)], axis=0) for _ in range(3)
    ]
    w_down = refs.pop(0)
    out_refs, router_part = refs[:-1], refs[-1]
    which = pl.program_id(0)
    router_add = dot_two(logit, x, TN)
    out = dot(hidden, w_down[0], NT).astype(BF)
    count = out.shape[0] // shards
    pick = slot_pick(count, count * per_device, capacity, which)
    total = count * per_device
    half = shards // 2
    parts = [
        (
            out_refs[index // half],
            slice(index % half * total, (index % half + 1) * total),
            dot(pick, out[mask * count : (mask + 1) * count], TN).astype(BF),
        )
        for index, mask in enumerate(doubling_order(shards))
    ]

    @pl.when(which == 0)
    def _():
        router_part[...] = router_add
        for ref, place, part in parts:
            ref[place, :] = part

    @pl.when(which > 0)
    def _():
        router_part[...] = router_part[...] + router_add
        for ref, place, part in parts:
            ref[place, :] = (ref[place, :].astype(F32) + part.astype(F32)).astype(BF)


def expert_weights_body(shards, *refs):
    refs = list(refs)
    x, up, hidden, pre = [
        jnp.concatenate([refs.pop(0)[0] for _ in range(shards)], axis=0) for _ in range(4)
    ]
    up_grad, down_grad = refs
    down_grad[0] = dot(up, hidden, TN)
    up_grad[0] = dot(x, pre, TN)


def norm_back(values, gain, grad):
    scale = lax.rsqrt(jnp.mean(values * values, axis=1, keepdims=True) + EPS)
    unit = values * scale
    inner = grad * gain
    gain_grad = jnp.sum(grad * unit, axis=0, keepdims=True)
    return scale * (inner - unit * jnp.mean(inner * unit, axis=1, keepdims=True)), gain_grad


def residual_body(sizes, ids, returned, back_slots, after, upstream, gains, ext, w_out, resid, resid_low, grad_ext, gain_part):
    heads, head_dim = sizes
    rows, width = after.shape
    grad = dot(back_slots[...], returned[...])
    value, part = norm_back(after[...], gains[1:2, :], grad)
    value = value + upstream[...].astype(F32)
    resid[...] = value
    resid_low[...] = value.astype(BF)
    gain_part[...] = part
    low = dot(value.astype(BF), w_out[...], NT).astype(BF)
    grad_ext[:, :width] = low
    product = low.astype(F32) * ext[:, :width].astype(F32)
    grad_ext[:, width:] = spread_parts(dot_two(product, member_rows(LANES, width, head_dim), NT))


def result_body(ids, returned, back_slots, after, gate, result):
    rows = dot(back_slots[...], returned[...]).astype(BF).astype(F32)
    result[...] = (after[...] + gate[:, :1] * rows).astype(BF)


def diagonal_parts(block, width):
    rows, keys = block.shape
    total = jnp.zeros((8, width), F32)
    for group in range(rows // 8):
        part = jnp.concatenate(
            [block[group * 8 : group * 8 + 8], jnp.zeros((8, width - keys), F32)], axis=1
        )
        total = total + pltpu.roll(part, rows - 8 - 8 * group, 1)
    return total


def spread_parts(values):
    high = values.astype(BF).astype(F32)
    middle = (values - high).astype(BF).astype(F32)
    low = (values - high - middle).astype(BF).astype(F32)
    return (high + pltpu.roll(middle, 32, 1) + pltpu.roll(low, 64, 1)).astype(BF)


def member_rows(head_rows, width, head_dim):
    head_of = lax.broadcasted_iota(jnp.int32, (head_rows, width), 1) // head_dim
    return (head_of == lax.broadcasted_iota(jnp.int32, (head_rows, width), 0)).astype(BF)


def part_rows(head_rows):
    part_of = lax.broadcasted_iota(jnp.int32, (head_rows, LANES), 1) % 32
    return (part_of == lax.broadcasted_iota(jnp.int32, (head_rows, LANES), 0)).astype(BF)


def query_body(sizes, ids, grad_ext, ext, joined_own, window, window_ref, keys_in, values_in, query_grad, table_part, delta, mass, diagonals):
    head_dim, buckets = sizes
    pair = pl.program_id(0)
    rows = ext.shape[0]
    width = ext.shape[1] - LANES
    keys = keys_in.shape[0]
    head_rows, span = window.shape

    @pl.when(pair == 0)
    def _():
        delta[...] = dot(grad_ext[:, width:], part_rows(head_rows), NT)
        mass[...] = dot(ext[:, width:], part_rows(head_rows), NT)

    head_lane = lax.broadcasted_iota(jnp.int32, (rows, head_rows), 1)

    def column_of(ref):
        return jnp.concatenate(
            [
                jnp.sum(jnp.where(head_lane == 2 * pair + k, ref[...], 0.0), axis=1, keepdims=True)
                for k in range(2)
            ],
            axis=0,
        )

    column = pl.multiple_of(pair * LANES, LANES)
    queries = pair_rows(joined_own[:, pl.ds(column, LANES)], head_dim)
    grad_own = pair_rows(grad_ext[:, pl.ds(column, LANES)], head_dim)
    scores = dot(queries, keys_in[...], NT) + jnp.concatenate(
        [bias_rows(window, 2 * pair + k, rows, keys) for k in range(2)], axis=0
    )
    probs = jnp.exp(scores - column_of(mass))
    score_grad = (probs * (dot(grad_own, values_in[...], NT) - column_of(delta))).astype(BF)
    query_grad[0] = pair_join(dot(score_grad, keys_in[...]), rows, head_dim).astype(BF)
    wide = score_grad.astype(F32)
    for k in range(2):
        start = pl.multiple_of((2 * pair + k) * 8, 8)
        diagonals[pl.ds(start, 8), :] = diagonal_parts(wide[k * rows : (k + 1) * rows], span)

    @pl.when(pair == pl.num_programs(0) - 1)
    def _():
        every = diagonals[...]
        total_rows = every.shape[0]
        lined = jnp.zeros((total_rows, span), F32)
        place = lax.broadcasted_iota(jnp.int32, (total_rows, span), 0) % 8
        for step in range(8):
            moved = every if step == 7 else pltpu.roll(every, 7 - step, 1)
            lined = jnp.where(place == step, moved, lined)
        line_rows = lax.broadcasted_iota(jnp.int32, (head_rows, total_rows), 1) // 8
        fold = (line_rows == lax.broadcasted_iota(jnp.int32, (head_rows, total_rows), 0)).astype(BF)
        high = lined.astype(BF)
        low = (lined - high.astype(F32)).astype(BF)
        sums = dot(fold, high) + dot(fold, low)
        table_part[...] = dot_two(sums, bucket_hot(window_ref, buckets), NT)


def key_body(sizes, *refs):
    devices, heads, head_dim = sizes
    refs = list(refs)
    ids = refs.pop(0)
    grad_pieces = [refs.pop(0) for _ in range(devices)]
    ext_pieces = [refs.pop(0) for _ in range(devices)]
    joined_own, mirror, query_grad, resid_low, queries_in = [refs.pop(0) for _ in range(5)]
    blocks, grads, delta_rows, mass_rows = refs
    expert_id = ids[0]
    pair = pl.program_id(0)
    rows, width = resid_low.shape
    keys = rows * devices
    head_rows = mirror.shape[0]
    pairs = heads // 2

    @pl.when(pair == 0)
    def _():
        place_blocks(grad_pieces, grads, expert_id)
        delta_rows[...] = dot(part_rows(head_rows), grads[:, width:], NT)
        for mask, piece in enumerate(ext_pieces):
            start = pl.multiple_of((expert_id ^ mask) * rows, rows)
            mass_rows[:, pl.ds(start, rows)] = dot(part_rows(head_rows), piece[:, width:], NT)
        blocks[:pairs] = query_grad[...]
        for block in range(pairs):
            blocks[3 * pairs + block] = resid_low[:, block * LANES : (block + 1) * LANES]
        for block in range(4 * pairs, blocks.shape[0]):
            blocks[block] = jnp.zeros((rows, LANES), BF)

    def row_of(ref):
        return jnp.concatenate(
            [jnp.broadcast_to(ref[pl.ds(2 * pair + k, 1), :], (rows, keys)) for k in range(2)],
            axis=0,
        )

    column = pl.multiple_of(pair * LANES, LANES)
    grad_all = grads[:, pl.ds(column, LANES)]
    key_own = pair_rows(joined_own[:, pl.ds(width + column, LANES)], head_dim)
    value_own = pair_rows(joined_own[:, pl.ds(2 * width + column, LANES)], head_dim)
    scores = dot(key_own, queries_in[...], NT) + jnp.concatenate(
        [bias_rows(mirror, 2 * pair + k, rows, keys) for k in range(2)], axis=0
    )
    probs = jnp.exp(scores - row_of(mass_rows))
    score_grad = (probs * (dot(value_own, grad_all, NT) - row_of(delta_rows))).astype(BF)
    blocks[pairs + pair] = pair_join(dot(score_grad, queries_in[...]), rows, head_dim).astype(BF)
    blocks[2 * pairs + pair] = pair_join(dot(probs.astype(BF), grad_all), rows, head_dim).astype(BF)


def source_body(shards, ids, *refs):
    refs = list(refs)
    tokens_grad, gain_part, joined, w_in, small = refs[-5:]
    blocks, tokens, gains, resid = refs[:4]
    place_weight(refs[4:-5], w_in, small, ids[0], ids[1], shards)
    for block in range(joined.shape[1] // LANES):
        joined[:, block * LANES : (block + 1) * LANES] = blocks[block]
    grad = dot(joined[...], w_in[...], NT)
    value, part = norm_back(tokens[...].astype(F32), gains[0:1, :], grad)
    tokens_grad[...] = (value + resid[...]).astype(BF)
    gain_part[...] = part


def weight_body(sizes, ids, xn_all, received, lines, *refs):
    per, pairs, shards = sizes
    devices, _, rows, _ = received.shape
    ext_pieces, parts, columns, mixed_all = refs[:devices], refs[devices:-2], refs[-2], refs[-1]
    width = xn_all.shape[1]
    rows_each = width // shards
    for source in range(devices):
        for block in range(per):
            columns[source * rows : (source + 1) * rows, block * LANES : (block + 1) * LANES] = received[
                source, block
            ]

    def store(value, line):
        for owner in range(shards):
            for mask in range(shards):

                @pl.when(ids[1] ^ mask == owner)
                def _():
                    parts[mask][:rows_each, line] = value[
                        owner * rows_each : (owner + 1) * rows_each
                    ].astype(BF)

    step = per if 3 * pairs % per == 0 else 1
    for block in range(0, per, step):
        inside = ids[0] * per + block < 3 * pairs
        line = slice(block * LANES, (block + step) * LANES)

        @pl.when(inside)
        def _():
            store(dot(xn_all[...], columns[:, line], TN), line)

        @pl.when(jnp.logical_not(inside))
        def _():
            for mask, piece in enumerate(ext_pieces):
                start = pl.multiple_of((ids[0] ^ mask) * rows, rows)
                mixed_all[pl.ds(start, rows), :] = piece[:, :width]
            store(dot(mixed_all[...], columns[:, line], TN), line)

    for mask in range(shards):
        parts[mask][rows_each:, :] = lines[ids[1] ^ mask]


def spread_body(sizes, ids, *refs):
    per, pairs = sizes
    pieces, (in_grad, out_grad, lines) = refs[:-3], refs[-3:]
    rows = in_grad.shape[0]
    total = None
    for mask, piece in enumerate(pieces):
        source = ids[0] ^ mask
        extra = piece[rows:, :].astype(F32)
        total = extra if total is None else total + extra
        for block in range(per):
            index = source * per + block
            values = piece[:rows, block * LANES : (block + 1) * LANES].astype(F32)

            @pl.when(index < 3 * pairs)
            def _():
                in_grad[:, pl.ds(pl.multiple_of(index * LANES, LANES), LANES)] = values

            @pl.when(jnp.logical_and(index >= 3 * pairs, index < 4 * pairs))
            def _():
                out_grad[:, pl.ds(pl.multiple_of((index - 3 * pairs) * LANES, LANES), LANES)] = values

    lines[...] = total


def pad_to(x, shape):
    return jnp.pad(x, [(0, size - have) for size, have in zip(shape, x.shape)])


def local(
    tokens, gain_attn, gain_mix, attn_in, attn_out, router, bias_table, expert_in, expert_down, routes, buckets, out_grad
):
    own_tokens = tokens[0]
    own_grad = out_grad[0]
    rows, width = own_tokens.shape
    devices = lax.axis_size("expert")
    shards = lax.axis_size("wshard")
    expert_id = lax.axis_index("expert")
    shard_id = lax.axis_index("wshard")
    heads = bias_table.shape[1]
    head_dim = width // heads
    experts = router.shape[1]
    bucket_count = bias_table.shape[0] * shards
    per_device = expert_in.shape[0]
    keys = rows * devices
    capacity = 3 * rows // (2 * experts)
    part = width // shards
    ids = jnp.stack([expert_id, shard_id]).astype(jnp.int32)

    table_rows = bias_table.shape[0]
    head_rows = 16
    small = jnp.concatenate(
        [
            router,
            gain_attn[:, None],
            gain_mix[:, None],
            pad_to(bias_table, (part, LANES - experts - 2)),
        ],
        axis=1,
    )
    in_chunks = weight_chunks(attn_in, small)
    chip_tokens = chip_pieces(own_tokens)
    window_width = keys + rows
    start = keys - 1 - expert_id * rows - (rows - 1)
    window_buckets = lax.dynamic_slice(jnp.pad(buckets, (0, rows)), (start,), (window_width,))
    mirror_buckets = lax.dynamic_slice(jnp.pad(buckets[::-1], (0, rows)), (start,), (window_width,))
    last = jnp.arange(window_width) == window_width - 1
    window_buckets = jnp.where(last, -1, window_buckets)[None]
    mirror_buckets = jnp.where(last, -1, mirror_buckets)[None]

    route = routes[0]
    earlier = jnp.arange(rows)[None, :] < jnp.arange(rows)[:, None]
    rank = jnp.sum(((route[None, :] == route[:, None]) & earlier).astype(jnp.int32), axis=1)
    slot = route * capacity + rank
    slot_count = experts * capacity
    slots = (jnp.arange(slot_count)[:, None] == slot[None, :]).astype(BF)
    back_slots = (slot[:, None] == jnp.arange(slot_count)[None, :]).astype(BF)
    chosen = (route[:, None] == jnp.arange(LANES)[None, :]).astype(BF)

    block = per_device * capacity

    def exchange(slot_rows):
        blocks = slot_rows.reshape(devices, block, width)
        moved = lax.all_to_all(blocks, "expert", split_axis=0, concat_axis=0, tiled=True)
        return moved.reshape(devices * block, width)

    def sum_back(parts):
        total = parts[0].astype(F32)
        for mask in range(1, shards):
            total = total + swap(parts[mask], "wshard", mask).astype(F32)
        return total.astype(BF)

    chip_tokens, in_chunks, attn_out, ups = tie(
        chip_tokens, in_chunks, attn_out, dot(slots, own_grad).astype(BF)
    )
    in_pieces = in_chunks
    if len(in_chunks) > 1:
        in_pieces = chip_pieces(jnp.concatenate(in_chunks, axis=0))
    token_pieces = core_pieces(chip_tokens)
    first_step, *later_steps = doubling_steps(shards)
    w_rows = swap(attn_out, "wshard", first_step)
    in_pieces, token_pieces, w_rows, ups, ids, window_buckets, mirror_buckets, chosen, slots, back_slots = tie(
        in_pieces,
        token_pieces,
        w_rows,
        exchange(ups),
        ids,
        window_buckets,
        mirror_buckets,
        chosen,
        slots,
        back_slots,
    )
    w_rows = jnp.concatenate([attn_out, w_rows], axis=0)
    for step in later_steps:
        w_rows = jnp.concatenate([w_rows, swap(w_rows, "wshard", step)], axis=0)
    ups_far = swap(ups, "wshard", first_step)
    if len(in_pieces) > 1:
        in_pieces = core_pieces(in_pieces)

    sizes = (devices, shards, heads, head_dim, bucket_count, experts, len(in_pieces))
    xn_all, joined, joined_own, ext, window, mirror, gains, router_pad = call(
        functools.partial(forward_body, sizes),
        [ids, *token_pieces, *in_pieces, window_buckets, mirror_buckets],
        [
            ((keys, width), BF),
            ((keys, 3 * width), BF),
            ((rows, 3 * width), BF),
            ((rows, width + LANES), BF),
            ((head_rows, window_width), F32),
            ((head_rows, window_width), F32),
            ((8, width), F32),
            ((width, LANES), BF),
        ],
        [
            pltpu.VMEM((keys, width), BF),
            pltpu.VMEM((keys, 3 * width), BF),
            pltpu.VMEM((width, 3 * width), BF),
            pltpu.SemaphoreType.DMA((2,)),
        ],
        far=(0, 1),
        name="attention_forward",
        us=0.2,
    )
    ups_far, w_rows, ext = tie(ups_far, w_rows, ext)
    ups_all = jnp.concatenate([ups, ups_far], axis=0)
    for step in later_steps:
        ups_all = jnp.concatenate([ups_all, swap(ups_all, "wshard", step)], axis=0)
    after, gate, send, w_out = call(
        functools.partial(route_body, (experts, shards)),
        [ids, w_rows, own_tokens, ext, gains, router_pad, chosen, slots],
        [((rows, width), F32), ((rows, LANES), F32), ((slot_count, width), BF), ((width, width), BF)],
        name="route",
        us=0.2,
    )
    rows_own = exchange(send)
    total = devices * block
    count = total // per_device
    ff = expert_in.shape[2]
    by_expert = pl.BlockSpec((1, width, ff), lambda k: (k, 0, 0))
    kept_ff = pl.BlockSpec((1, count, ff), lambda k: (k, 0, 0))
    kept_width = pl.BlockSpec((1, count, width), lambda k: (k, 0, 0))
    kept_lanes = pl.BlockSpec((1, count, LANES), lambda k: (k, 0, 0))
    upstream_width = pl.BlockSpec((1, shards * count, width), lambda k: (k, 0, 0))
    upstream_ff = pl.BlockSpec((1, shards * count, ff), lambda k: (k, 0, 0))
    ups_all, rows_own = tie(ups_all, rows_own)
    row_chunks = {0: rows_own}
    steps = [1 << bit for bit in reversed(range((shards - 1).bit_length()))]
    row_chunks.update({step: swap(rows_own, "wshard", step) for step in steps})
    ups_all, spread_all = pl.pallas_call(
        functools.partial(upstream_body, (shards, per_device, capacity)),
        grid=(per_device,),
        in_specs=[whole((shards * total, width)), by_expert],
        out_specs=[upstream_width, upstream_ff],
        out_shape=[
            jax.ShapeDtypeStruct((per_device, shards * count, width), BF),
            jax.ShapeDtypeStruct((per_device, shards * count, ff), F32),
        ],
        compiler_params=pltpu.CompilerParams(vmem_limit_bytes=VMEM_BYTES),
        cost_estimate=cost(0.001),
        name="upstream",
    )(ups_all, expert_down)
    ext_later, _ = tie(ext, rows_own)
    ext_pieces = core_pieces(chip_pieces(ext_later))
    kept = [[], [], [], [], []]
    back_parts = []
    for step in range(shards):
        row_chunk = row_chunks[step]
        if step:
            row_chunk, _ = tie(row_chunk, back_parts[-1])
        back, *saved = pl.pallas_call(
            functools.partial(expert_body, (experts, per_device, capacity)),
            grid=(per_device,),
            in_specs=[
                pl.BlockSpec(memory_space=pltpu.SMEM),
                whole((total, width)),
                pl.BlockSpec((1, count, width), lambda k, step=step: (k, step, 0)),
                pl.BlockSpec((1, count, ff), lambda k, step=step: (k, step, 0)),
                by_expert,
                whole((width, LANES)),
            ],
            out_specs=[whole((total, width)), kept_width, kept_width, kept_ff, kept_ff, kept_lanes],
            out_shape=[
                jax.ShapeDtypeStruct((total, width), BF),
                jax.ShapeDtypeStruct((per_device, count, width), BF),
                jax.ShapeDtypeStruct((per_device, count, width), BF),
                jax.ShapeDtypeStruct((per_device, count, ff), BF),
                jax.ShapeDtypeStruct((per_device, count, ff), BF),
                jax.ShapeDtypeStruct((per_device, count, LANES), F32),
            ],
            compiler_params=pltpu.CompilerParams(vmem_limit_bytes=VMEM_BYTES),
            cost_estimate=cost(0.001),
            name="experts",
        )(ids, row_chunk, ups_all, spread_all, expert_in, router_pad)
        back_parts.append(back)
        for group, value in zip(kept, saved):
            group.append(value)
        if step == 1:
            for mask in range(1, shards):
                nearer = mask & (-mask)
                if mask != nearer:
                    value, _ = tie(row_chunks[mask ^ nearer], back)
                    row_chunks[mask] = swap(value, "wshard", nearer)
    kept, back_sum = tie(kept, sum_back(back_parts))
    returned_grad = exchange(back_sum)
    out_near, out_far, router_part = pl.pallas_call(
        functools.partial(expert_out_body, (shards, per_device, capacity)),
        grid=(per_device,),
        in_specs=[kept_width] * shards + [kept_ff] * shards + [kept_lanes] * shards + [by_expert],
        out_specs=[whole((shards // 2 * total, width))] * 2 + [whole((LANES, width))],
        out_shape=[jax.ShapeDtypeStruct((shards // 2 * total, width), BF)] * 2
        + [jax.ShapeDtypeStruct((LANES, width), F32)],
        compiler_params=pltpu.CompilerParams(vmem_limit_bytes=VMEM_BYTES),
        cost_estimate=cost(5.0),
        name="expert_out",
    )(*kept[0], *kept[2], *kept[4], expert_down)
    out_near, out_far, router_part, returned_grad = tie(out_near, out_far, router_part, returned_grad)
    out_sum = (out_near.astype(F32) + swap(out_far, "wshard", 1).astype(F32)).astype(BF)
    resid, resid_low, grad_ext, gain_two_part = call(
        functools.partial(residual_body, (heads, head_dim)),
        [ids, returned_grad, back_slots, after, own_grad, gains, ext, w_out],
        [((rows, width), F32), ((rows, width), BF), ((rows, width + LANES), BF), ((1, width), F32)],
        name="residual",
        us=2.0,
    )
    grad_pieces = chip_pieces(grad_ext)
    pairs = heads // 2

    def column_block(offset):
        return pl.BlockSpec((keys, LANES), lambda p: (0, offset * pairs + p))

    query_grad, table_part = pl.pallas_call(
        functools.partial(query_body, (head_dim, bucket_count)),
        grid=(pairs,),
        in_specs=[
            pl.BlockSpec(memory_space=pltpu.SMEM),
            whole((rows, width + LANES)),
            whole((rows, width + LANES)),
            whole((rows, 3 * width)),
            whole((head_rows, window_width)),
            whole((1, window_width)),
            column_block(1),
            column_block(2),
        ],
        out_specs=[pl.BlockSpec((1, rows, LANES), lambda p: (p, 0, 0)), whole((head_rows, bucket_count))],
        out_shape=[
            jax.ShapeDtypeStruct((pairs, rows, LANES), BF),
            jax.ShapeDtypeStruct((head_rows, bucket_count), F32),
        ],
        scratch_shapes=[
            pltpu.VMEM((rows, head_rows), F32),
            pltpu.VMEM((rows, head_rows), F32),
            pltpu.VMEM((head_rows * 8, window_width), F32),
        ],
        compiler_params=pltpu.CompilerParams(vmem_limit_bytes=VMEM_BYTES),
        cost_estimate=cost(10.0),
        name="query_grad",
    )(ids, grad_ext, ext, joined_own, window, window_buckets, joined, joined)
    per = -(-4 * pairs // devices)
    grad_pieces, query_grad = tie(grad_pieces, query_grad)
    grad_pieces = core_pieces(grad_pieces)
    (blocks,) = pl.pallas_call(
        functools.partial(key_body, (devices, heads, head_dim)),
        grid=(pairs,),
        in_specs=[pl.BlockSpec(memory_space=pltpu.SMEM)]
        + [whole((rows, width + LANES))] * (2 * devices)
        + [
            whole((rows, 3 * width)),
            whole((head_rows, window_width)),
            whole((pairs, rows, LANES)),
            whole((rows, width)),
            column_block(0),
        ],
        out_specs=[whole((per * devices, rows, LANES))],
        out_shape=[
            jax.ShapeDtypeStruct((per * devices, rows, LANES), BF),
        ],
        scratch_shapes=[
            pltpu.VMEM((keys, width + LANES), BF),
            pltpu.VMEM((head_rows, keys), F32),
            pltpu.VMEM((head_rows, keys), F32),
        ],
        compiler_params=pltpu.CompilerParams(vmem_limit_bytes=VMEM_BYTES),
        cost_estimate=cost(12.0),
        name="key_grad",
    )(ids, *grad_pieces, *ext_pieces, joined_own, mirror, query_grad, resid_low, joined)
    for step in reversed(doubling_steps(shards)[:-1]):
        half = out_sum.shape[0] // 2
        moved = swap(out_sum[half:], "wshard", step)
        out_sum = (out_sum[:half].astype(F32) + moved.astype(F32)).astype(BF)
    received = lax.all_to_all(
        blocks.reshape(devices, per, rows, LANES), "expert", split_axis=0, concat_axis=0, tiled=True
    )
    tokens_grad, gain_one_part = call(
        functools.partial(source_body, shards),
        [ids, blocks, own_tokens, gains, resid, *in_pieces],
        [((rows, width), BF), ((1, width), F32)],
        [
            pltpu.VMEM((rows, 3 * width), BF),
            pltpu.VMEM((width, 3 * width), BF),
            pltpu.VMEM((width, LANES), BF),
        ],
        name="source_grad",
        us=4.0,
    )
    table_line = table_part[:heads].T.reshape(shards, table_rows * heads)
    table_line = pad_to(table_line, (shards, part)).reshape(1, width)
    lines = jnp.concatenate([router_part[:experts], gain_one_part, gain_two_part, table_line], axis=0)
    line_count = lines.shape[0]
    groups = per * LANES // part
    line_rows = -(-line_count // (16 * groups)) * 16
    lines = pad_to(lines, (groups * line_rows, width)).reshape(groups, line_rows, shards, part)
    lines = lines.transpose(2, 1, 0, 3).reshape(shards, line_rows, groups * part)
    lines = pad_to(lines, (shards, line_rows, per * LANES)).astype(BF)
    weight_parts = call(
        functools.partial(weight_body, (per, pairs, shards)),
        [ids, xn_all, received, lines, *ext_pieces],
        [((part + line_rows, per * LANES), BF)] * shards,
        [pltpu.VMEM((keys, per * LANES), BF), pltpu.VMEM((keys, width), BF)],
        name="weight_grads",
        us=4.0,
    )
    weight_parts, out_sum, kept = tie(weight_parts, out_sum, kept)
    up_grad, down_grad = pl.pallas_call(
        functools.partial(expert_weights_body, shards),
        grid=(per_device,),
        in_specs=[kept_width] * (2 * shards) + [kept_ff] * (2 * shards),
        out_specs=[by_expert, by_expert],
        out_shape=[jax.ShapeDtypeStruct((per_device, width, ff), F32)] * 2,
        compiler_params=pltpu.CompilerParams(vmem_limit_bytes=VMEM_BYTES),
        cost_estimate=cost(7.0),
        name="expert_weights",
    )(*kept[0], *kept[1], *kept[2], *kept[3])
    mine = sum_back(weight_parts)
    returned_rows = exchange(out_sum)
    mine, returned_rows, up_grad, down_grad = tie(mine, returned_rows, up_grad, down_grad)
    pieces = chip_pieces(mine)
    (result,) = call(
        result_body,
        [ids, returned_rows, back_slots, after, gate],
        [((rows, width), BF)],
        name="result",
        us=2.0,
    )
    pieces, result = tie(pieces, result)
    attn_in_grad, attn_out_grad, lines = call(
        functools.partial(spread_body, (per, pairs)),
        [ids, *core_pieces(pieces)],
        [((part, 3 * width), F32), ((part, width), F32), ((line_rows, per * LANES), F32)],
        name="spread",
        us=2.0,
    )
    lines = lines[:, : groups * part].reshape(line_rows, groups, part).transpose(1, 0, 2)
    lines = lines.reshape(groups * line_rows, part)
    router_grad = lines[:experts].T
    table_grad = lines[experts + 2, : table_rows * heads].reshape(table_rows, heads)
    return (
        result[None],
        tokens_grad[None],
        lines[experts],
        lines[experts + 1],
        attn_in_grad,
        attn_out_grad,
        router_grad,
        table_grad,
        up_grad,
        down_grad,
    )


def solution(mesh):
    return jax.shard_map(
        local,
        mesh=mesh,
        in_specs=(
            P("wshard", "expert", None),
            P("wshard"),
            P("wshard"),
            P("wshard", None),
            P("wshard", None),
            P("wshard", None),
            P("wshard", None),
            P("expert", None, "wshard"),
            P("expert", None, "wshard"),
            P("wshard", "expert"),
            P(),
            P("wshard", "expert", None),
        ),
        out_specs=(
            P("wshard", "expert", None),
            P("wshard", "expert", None),
            P("wshard"),
            P("wshard"),
            P("wshard", None),
            P("wshard", None),
            P("wshard", None),
            P("wshard", None),
            P("expert", None, "wshard"),
            P("expert", None, "wshard"),
        ),
        check_vma=False,
    )
```

```python
import functools

import jax
import jax.numpy as jnp
from jax import lax
from jax.experimental import pallas as pl
from jax.experimental.pallas import tpu as pltpu
from jax.sharding import PartitionSpec as P

BF = jnp.bfloat16
F32 = jnp.float32
EPS = 1e-06
LANES = 128
VMEM_BYTES = 60 * 1024 * 1024
NN = (((1,), (0,)), ((), ()))
NT = (((1,), (1,)), ((), ()))
TN = (((0,), (0,)), ((), ()))


def dot(a, b, dims=NN):
    return lax.dot_general(a, b, dims, preferred_element_type=F32)


def dot_two(a, b, dims=NN):
    high = a.astype(BF)
    low = (a - high.astype(F32)).astype(BF)
    return dot(high, b, dims) + dot(low, b, dims)


def swap(x, axis, mask):
    count = lax.axis_size(axis)
    return lax.ppermute(x, axis, [(i, i ^ mask) for i in range(count)])


def tie(*groups):
    return lax.optimization_barrier(groups)


def chip_pieces(x):
    return [x] + [swap(x, "expert", mask) for mask in range(2, lax.axis_size("expert"), 2)]


def core_pieces(pieces):
    return [block for piece in pieces for block in (piece, swap(piece, "expert", 1))]


def weight_chunks(shard, small):
    rows, columns = shard.shape
    chips = lax.axis_size("expert") // 2
    if rows % (16 * chips) or columns % (2 * LANES):
        return [lax.all_gather(jnp.concatenate([shard, small], axis=1), "wshard", axis=0, tiled=True)]
    mine = lax.axis_index("expert")
    first = mine // 2 * (rows // chips)
    chunk = lax.dynamic_slice(shard, (first, mine % 2 * (columns // 2)), (rows // chips, columns // 2))
    beside = lax.dynamic_slice(small, (first, 0), (rows // chips, small.shape[1]))
    chunk = jnp.concatenate([chunk, beside], axis=1)
    return [chunk] + [swap(chunk, "wshard", mask) for mask in range(1, lax.axis_size("wshard"))]


def doubling_steps(count):
    return [1 << bit for bit in reversed(range((count - 1).bit_length()))]


def doubling_order(count):
    order = [0]
    for step in doubling_steps(count):
        order = order + [mask ^ step for mask in order]
    return order


def place_order(gathered, target, shard_id, shards):
    rows = target.shape[0] // shards
    for index, mask in enumerate(doubling_order(shards)):
        row = pl.multiple_of((shard_id ^ mask) * rows, 16)
        target[pl.ds(row, rows), :] = gathered[index * rows : (index + 1) * rows, :]


def place_weight(pieces, target, small, expert_id, shard_id, shards):
    rows, columns = target.shape
    if len(pieces) == 1:
        target[...] = pieces[0][:, :columns]
        small[...] = pieces[0][:, columns:]
        return
    chips = len(pieces) // 2
    chunk = rows // shards // chips
    for mask, piece in enumerate(pieces):
        source = expert_id ^ mask
        column = pl.multiple_of(source % 2 * (columns // 2), LANES)
        for step in range(shards):
            row = (shard_id ^ step) * (rows // shards) + source // 2 * chunk
            row = pl.multiple_of(row, 16)
            lines = slice(step * chunk, (step + 1) * chunk)
            target[pl.ds(row, chunk), pl.ds(column, columns // 2)] = piece[lines, : columns // 2]
            if mask % 2 == 0:
                small[pl.ds(row, chunk), :] = piece[lines, columns // 2 :]


def place_blocks(pieces, target, expert_id, change=None):
    for mask, piece in enumerate(pieces):
        count = piece.shape[0]
        start = pl.multiple_of((expert_id ^ mask) * count, count)
        block = piece[...]
        target[pl.ds(start, count), :] = block if change is None else change(block)


def bias_rows(window, head, rows, keys):
    row = window[pl.ds(head, 1), :]
    width = row.shape[1]
    spread = jnp.broadcast_to(row, (rows, width))
    return pltpu.roll(spread, width - (rows - 1), 1, stride=1, stride_axis=0)[:, :keys]


def pair_rows(block, head_dim):
    lane = lax.broadcasted_iota(jnp.int32, block.shape, 1)
    zero = jnp.zeros_like(block)
    return jnp.concatenate(
        [jnp.where(lane < head_dim, block, zero), jnp.where(lane < head_dim, zero, block)], axis=0
    )


def pair_join(both, rows, head_dim):
    lane = lax.broadcasted_iota(jnp.int32, (rows, both.shape[1]), 1)
    return jnp.where(lane < head_dim, both[:rows], both[rows:])


def bucket_hot(window_ref, buckets):
    width = window_ref.shape[1]
    index = lax.broadcasted_iota(jnp.int32, (buckets, width), 0)
    return (index == window_ref[...]).astype(BF)


def whole(shape):
    return pl.BlockSpec(shape, lambda *_: (0,) * len(shape))


def call(body, args, outs, scratch=(), name=None, us=1.0, far=()):
    ids = pl.BlockSpec(memory_space=pltpu.SMEM)
    near = pl.BlockSpec(memory_space=pltpu.VMEM)
    return pl.pallas_call(
        body,
        in_specs=[ids] + [near] * (len(args) - 1),
        out_specs=[pl.BlockSpec(memory_space=pl.ANY) if k in far else near for k in range(len(outs))],
        out_shape=[jax.ShapeDtypeStruct(shape, kind) for shape, kind in outs],
        scratch_shapes=list(scratch),
        compiler_params=pltpu.CompilerParams(vmem_limit_bytes=VMEM_BYTES),
        cost_estimate=cost(us),
        name=name,
    )(*args)


def cost(us):
    return pl.CostEstimate(flops=int(us * 1e9), bytes_accessed=int(us * 1e6), transcendentals=0)


def normalize(block, gain):
    values = block.astype(F32)
    scale = lax.rsqrt(jnp.mean(values * values, axis=1, keepdims=True) + EPS)
    return (values * scale * gain).astype(BF)


def forward_body(sizes, *refs):
    devices, shards, heads, head_dim, buckets, experts, in_count = sizes
    refs = list(refs)
    ids = refs.pop(0)
    tokens = [refs.pop(0) for _ in range(devices)]
    in_pieces = [refs.pop(0) for _ in range(in_count)]
    window_ref, mirror_ref = [refs.pop(0) for _ in range(2)]
    xn_far, joined_far, joined_own, ext, window, mirror, gains, small, xn_all, joined, w_in, sems = refs
    expert_id = ids[0]
    shard_id = ids[1]
    rows, width = tokens[0].shape
    keys = rows * devices
    place_weight(in_pieces, w_in, small, expert_id, shard_id, shards)
    turned = small[...].astype(F32).T
    gains[...] = turned[experts : experts + 8, :]
    gain_one = gains[0:1, :]
    place_blocks(tokens, xn_all, expert_id, lambda block: normalize(block, gain_one))
    xn_copy = pltpu.make_async_copy(xn_all, xn_far, sems.at[0])
    xn_copy.start()
    head_rows = window.shape[0]
    per_shard = buckets // shards
    spot = lax.broadcasted_iota(jnp.int32, (buckets, width), 1)
    bucket = lax.broadcasted_iota(jnp.int32, (buckets, width), 0)
    spot_hot = (spot == bucket // per_shard * (width // shards) + bucket % per_shard).astype(BF)
    table = dot(turned[experts + 2 : experts + 2 + head_rows, :].astype(BF), spot_hot, NT).astype(BF)
    column_block = 2 * LANES
    row_block = min(1024, keys)

    def project(step, carry):
        row = pl.multiple_of(step // (3 * width // column_block) * row_block, row_block)
        column = pl.multiple_of(step % (3 * width // column_block) * column_block, column_block)
        joined[pl.ds(row, row_block), pl.ds(column, column_block)] = dot(
            xn_all[pl.ds(row, row_block), :], w_in[:, pl.ds(column, column_block)]
        ).astype(BF)
        return carry

    lax.fori_loop(0, (3 * width // column_block) * (keys // row_block), project, 0)
    joined_copy = pltpu.make_async_copy(joined, joined_far, sems.at[1])
    joined_copy.start()
    window[...] = dot(table, bucket_hot(window_ref, buckets))
    mirror[...] = dot(table, bucket_hot(mirror_ref, buckets))
    own = pl.multiple_of(expert_id * rows, rows)
    joined_own[...] = joined[pl.ds(own, rows), :]
    lane = lax.broadcasted_iota(jnp.int32, (rows, LANES), 1)

    def attend(pair, masses):
        column = pl.multiple_of(pair * LANES, LANES)
        queries = pair_rows(joined_own[:, pl.ds(column, LANES)], head_dim)
        scores = dot(queries, joined[:, pl.ds(width + column, LANES)], NT)
        scores = scores + jnp.concatenate(
            [bias_rows(window, 2 * pair + k, rows, keys) for k in range(2)], axis=0
        )
        top = jnp.max(scores, axis=1, keepdims=True)
        probs = jnp.exp(scores - top)
        mass = jnp.sum(probs, axis=1, keepdims=True)
        mixed = dot(probs.astype(BF), joined[:, pl.ds(2 * width + column, LANES)]) / mass
        ext[:, pl.ds(column, LANES)] = pair_join(mixed, rows, head_dim).astype(BF)
        total = top + jnp.log(mass)
        masses = jnp.where(lane == 2 * pair, total[:rows], masses)
        return jnp.where(lane == 2 * pair + 1, total[rows:], masses)

    masses = lax.fori_loop(0, heads // 2, attend, jnp.zeros((rows, LANES), F32))
    ext[:, width:] = spread_parts(masses)
    xn_copy.wait()
    joined_copy.wait()


def route_body(sizes, ids, w_rows, tokens, ext, gains, router, chosen, slots, after, gate, send, w_out):
    experts, shards = sizes
    rows, width = tokens.shape
    place_order(w_rows, w_out, ids[1], shards)
    lane = lax.broadcasted_iota(jnp.int32, (rows, LANES), 1)
    post = tokens[...].astype(F32) + dot(ext[:, :width], w_out[...])
    after[...] = post
    xn_two = normalize(post, gains[1:2, :])
    logits = jnp.where(lane < experts, dot(xn_two, router[...]), -1e30)
    weights = jnp.exp(logits - jnp.max(logits, axis=1, keepdims=True))
    weights = weights / jnp.sum(weights, axis=1, keepdims=True)
    gate[...] = jnp.broadcast_to(
        jnp.sum(weights * chosen[...].astype(F32), axis=1, keepdims=True), (rows, LANES)
    )
    send[...] = dot(slots[...], xn_two).astype(BF)


def slot_pick(count, total, capacity, which):
    row = lax.broadcasted_iota(jnp.int32, (count, total), 0)
    column = lax.broadcasted_iota(jnp.int32, (count, total), 1)
    block = total // count * capacity
    return (column == row // capacity * block + which * capacity + row % capacity).astype(BF)


def upstream_body(sizes, chunks, w_down, up_ref, spread_ref):
    shards, per_device, capacity = sizes
    total = chunks.shape[0] // shards
    count = total // per_device
    pick = slot_pick(count, total, capacity, pl.program_id(0))
    for index, mask in enumerate(doubling_order(shards)):
        chunk = chunks[index * total : (index + 1) * total, :]
        up_ref[0, mask * count : (mask + 1) * count, :] = dot(pick, chunk).astype(BF)
    spread_ref[0] = dot(up_ref[0], w_down[0])


def expert_body(sizes, ids, rows_in, ups_in, spread_in, w_up, router, back_ref, x_ref, up_ref, hidden_ref, pre_ref, logit_ref):
    experts, per_device, capacity = sizes
    which = pl.program_id(0)
    mine = ids[0] * per_device + which
    total = rows_in.shape[0]
    count = total // per_device
    pick = slot_pick(count, total, capacity, which)
    x = dot(pick, rows_in[...]).astype(BF)
    lane = lax.broadcasted_iota(jnp.int32, (count, LANES), 1)
    logits = jnp.where(lane < experts, dot(x, router[...]), -1e30)
    probs = jnp.exp(logits - jnp.max(logits, axis=1, keepdims=True))
    probs = probs / jnp.sum(probs, axis=1, keepdims=True)
    hot = (lane == mine).astype(F32)
    gate = jnp.sum(probs * hot, axis=1, keepdims=True)
    pre = dot(x, w_up[0])
    inner = 0.7978845608028654 * (pre + 0.044715 * pre * pre * pre)
    bend = jnp.tanh(inner)
    hidden = 0.5 * pre * (1.0 + bend)
    slope = 0.5 * (1.0 + bend) + 0.5 * pre * (1.0 - bend * bend) * (
        0.7978845608028654 * (1.0 + 3.0 * 0.044715 * pre * pre)
    )
    hidden_low = hidden.astype(BF)
    spread = spread_in[0]
    gate_part = jnp.sum(hidden_low.astype(F32) * spread, axis=1, keepdims=True)
    pre_grad = (gate * spread * slope).astype(BF)
    logit_grad = gate_part * probs * (hot - gate)
    back = dot(pre_grad, w_up[0], NT) + dot_two(logit_grad, router[...], NT)
    x_ref[0] = x
    up_ref[0] = (gate * ups_in[0].astype(F32)).astype(BF)
    hidden_ref[0] = hidden_low
    pre_ref[0] = pre_grad
    logit_ref[0] = logit_grad
    back = dot(pick, back.astype(BF), TN).astype(BF)

    @pl.when(which == 0)
    def _():
        back_ref[...] = back

    @pl.when(which > 0)
    def _():
        back_ref[...] = (back_ref[...].astype(F32) + back.astype(F32)).astype(BF)


def expert_out_body(sizes, *refs):
    shards, per_device, capacity = sizes
    refs = list(refs)
    x, hidden, logit = [
        jnp.concatenate([refs.pop(0)[0] for _ in range(shards)], axis=0) for _ in range(3)
    ]
    w_down = refs.pop(0)
    out_refs, router_part = refs[:-1], refs[-1]
    which = pl.program_id(0)
    router_add = dot_two(logit, x, TN)
    out = dot(hidden, w_down[0], NT).astype(BF)
    count = out.shape[0] // shards
    pick = slot_pick(count, count * per_device, capacity, which)
    total = count * per_device
    half = shards // 2
    parts = [
        (
            out_refs[index // half],
            slice(index % half * total, (index % half + 1) * total),
            dot(pick, out[mask * count : (mask + 1) * count], TN).astype(BF),
        )
        for index, mask in enumerate(doubling_order(shards))
    ]

    @pl.when(which == 0)
    def _():
        router_part[...] = router_add
        for ref, place, part in parts:
            ref[place, :] = part

    @pl.when(which > 0)
    def _():
        router_part[...] = router_part[...] + router_add
        for ref, place, part in parts:
            ref[place, :] = (ref[place, :].astype(F32) + part.astype(F32)).astype(BF)


def expert_weights_body(shards, *refs):
    refs = list(refs)
    x, up, hidden, pre = [
        jnp.concatenate([refs.pop(0)[0] for _ in range(shards)], axis=0) for _ in range(4)
    ]
    up_grad, down_grad = refs
    down_grad[0] = dot(up, hidden, TN)
    up_grad[0] = dot(x, pre, TN)


def norm_back(values, gain, grad):
    scale = lax.rsqrt(jnp.mean(values * values, axis=1, keepdims=True) + EPS)
    unit = values * scale
    inner = grad * gain
    gain_grad = jnp.sum(grad * unit, axis=0, keepdims=True)
    return scale * (inner - unit * jnp.mean(inner * unit, axis=1, keepdims=True)), gain_grad


def residual_body(sizes, ids, returned, back_slots, after, upstream, gains, ext, w_out, resid, resid_low, grad_ext, gain_part):
    heads, head_dim = sizes
    rows, width = after.shape
    grad = dot(back_slots[...], returned[...])
    value, part = norm_back(after[...], gains[1:2, :], grad)
    value = value + upstream[...].astype(F32)
    resid[...] = value
    resid_low[...] = value.astype(BF)
    gain_part[...] = part
    low = dot(value.astype(BF), w_out[...], NT).astype(BF)
    grad_ext[:, :width] = low
    product = low.astype(F32) * ext[:, :width].astype(F32)
    grad_ext[:, width:] = spread_parts(dot_two(product, member_rows(LANES, width, head_dim), NT))


def result_body(ids, returned, back_slots, after, gate, result):
    rows = dot(back_slots[...], returned[...]).astype(BF).astype(F32)
    result[...] = (after[...] + gate[:, :1] * rows).astype(BF)


def diagonal_parts(block, width):
    rows, keys = block.shape
    total = jnp.zeros((8, width), F32)
    for group in range(rows // 8):
        part = jnp.concatenate(
            [block[group * 8 : group * 8 + 8], jnp.zeros((8, width - keys), F32)], axis=1
        )
        total = total + pltpu.roll(part, rows - 8 - 8 * group, 1)
    return total


def spread_parts(values):
    high = values.astype(BF).astype(F32)
    middle = (values - high).astype(BF).astype(F32)
    low = (values - high - middle).astype(BF).astype(F32)
    return (high + pltpu.roll(middle, 32, 1) + pltpu.roll(low, 64, 1)).astype(BF)


def member_rows(head_rows, width, head_dim):
    head_of = lax.broadcasted_iota(jnp.int32, (head_rows, width), 1) // head_dim
    return (head_of == lax.broadcasted_iota(jnp.int32, (head_rows, width), 0)).astype(BF)


def part_rows(head_rows):
    part_of = lax.broadcasted_iota(jnp.int32, (head_rows, LANES), 1) % 32
    return (part_of == lax.broadcasted_iota(jnp.int32, (head_rows, LANES), 0)).astype(BF)


def query_body(sizes, ids, grad_ext, ext, joined_own, window, window_ref, keys_in, values_in, query_grad, table_part, delta, mass, diagonals):
    head_dim, buckets = sizes
    pair = pl.program_id(0)
    rows = ext.shape[0]
    width = ext.shape[1] - LANES
    keys = keys_in.shape[0]
    head_rows, span = window.shape

    @pl.when(pair == 0)
    def _():
        delta[...] = dot(grad_ext[:, width:], part_rows(head_rows), NT)
        mass[...] = dot(ext[:, width:], part_rows(head_rows), NT)

    head_lane = lax.broadcasted_iota(jnp.int32, (rows, head_rows), 1)

    def column_of(ref):
        return jnp.concatenate(
            [
                jnp.sum(jnp.where(head_lane == 2 * pair + k, ref[...], 0.0), axis=1, keepdims=True)
                for k in range(2)
            ],
            axis=0,
        )

    column = pl.multiple_of(pair * LANES, LANES)
    queries = pair_rows(joined_own[:, pl.ds(column, LANES)], head_dim)
    grad_own = pair_rows(grad_ext[:, pl.ds(column, LANES)], head_dim)
    scores = dot(queries, keys_in[...], NT) + jnp.concatenate(
        [bias_rows(window, 2 * pair + k, rows, keys) for k in range(2)], axis=0
    )
    probs = jnp.exp(scores - column_of(mass))
    score_grad = (probs * (dot(grad_own, values_in[...], NT) - column_of(delta))).astype(BF)
    query_grad[0] = pair_join(dot(score_grad, keys_in[...]), rows, head_dim).astype(BF)
    wide = score_grad.astype(F32)
    for k in range(2):
        start = pl.multiple_of((2 * pair + k) * 8, 8)
        diagonals[pl.ds(start, 8), :] = diagonal_parts(wide[k * rows : (k + 1) * rows], span)

    @pl.when(pair == pl.num_programs(0) - 1)
    def _():
        every = diagonals[...]
        total_rows = every.shape[0]
        lined = jnp.zeros((total_rows, span), F32)
        place = lax.broadcasted_iota(jnp.int32, (total_rows, span), 0) % 8
        for step in range(8):
            moved = every if step == 7 else pltpu.roll(every, 7 - step, 1)
            lined = jnp.where(place == step, moved, lined)
        line_rows = lax.broadcasted_iota(jnp.int32, (head_rows, total_rows), 1) // 8
        fold = (line_rows == lax.broadcasted_iota(jnp.int32, (head_rows, total_rows), 0)).astype(BF)
        high = lined.astype(BF)
        low = (lined - high.astype(F32)).astype(BF)
        sums = dot(fold, high) + dot(fold, low)
        table_part[...] = dot_two(sums, bucket_hot(window_ref, buckets), NT)


def key_body(sizes, *refs):
    devices, heads, head_dim = sizes
    refs = list(refs)
    ids = refs.pop(0)
    grad_pieces = [refs.pop(0) for _ in range(devices)]
    ext_pieces = [refs.pop(0) for _ in range(devices)]
    joined_own, mirror, query_grad, resid_low, queries_in = [refs.pop(0) for _ in range(5)]
    blocks, grads, delta_rows, mass_rows = refs
    expert_id = ids[0]
    pair = pl.program_id(0)
    rows, width = resid_low.shape
    keys = rows * devices
    head_rows = mirror.shape[0]
    pairs = heads // 2

    @pl.when(pair == 0)
    def _():
        place_blocks(grad_pieces, grads, expert_id)
        delta_rows[...] = dot(part_rows(head_rows), grads[:, width:], NT)
        for mask, piece in enumerate(ext_pieces):
            start = pl.multiple_of((expert_id ^ mask) * rows, rows)
            mass_rows[:, pl.ds(start, rows)] = dot(part_rows(head_rows), piece[:, width:], NT)
        blocks[:pairs] = query_grad[...]
        for block in range(pairs):
            blocks[3 * pairs + block] = resid_low[:, block * LANES : (block + 1) * LANES]
        for block in range(4 * pairs, blocks.shape[0]):
            blocks[block] = jnp.zeros((rows, LANES), BF)

    def row_of(ref):
        return jnp.concatenate(
            [jnp.broadcast_to(ref[pl.ds(2 * pair + k, 1), :], (rows, keys)) for k in range(2)],
            axis=0,
        )

    column = pl.multiple_of(pair * LANES, LANES)
    grad_all = grads[:, pl.ds(column, LANES)]
    key_own = pair_rows(joined_own[:, pl.ds(width + column, LANES)], head_dim)
    value_own = pair_rows(joined_own[:, pl.ds(2 * width + column, LANES)], head_dim)
    scores = dot(key_own, queries_in[...], NT) + jnp.concatenate(
        [bias_rows(mirror, 2 * pair + k, rows, keys) for k in range(2)], axis=0
    )
    probs = jnp.exp(scores - row_of(mass_rows))
    score_grad = (probs * (dot(value_own, grad_all, NT) - row_of(delta_rows))).astype(BF)
    blocks[pairs + pair] = pair_join(dot(score_grad, queries_in[...]), rows, head_dim).astype(BF)
    blocks[2 * pairs + pair] = pair_join(dot(probs.astype(BF), grad_all), rows, head_dim).astype(BF)


def source_body(shards, ids, *refs):
    refs = list(refs)
    tokens_grad, gain_part, joined, w_in, small = refs[-5:]
    blocks, tokens, gains, resid = refs[:4]
    place_weight(refs[4:-5], w_in, small, ids[0], ids[1], shards)
    for block in range(joined.shape[1] // LANES):
        joined[:, block * LANES : (block + 1) * LANES] = blocks[block]
    grad = dot(joined[...], w_in[...], NT)
    value, part = norm_back(tokens[...].astype(F32), gains[0:1, :], grad)
    tokens_grad[...] = (value + resid[...]).astype(BF)
    gain_part[...] = part


def weight_body(sizes, ids, xn_all, received, lines, *refs):
    per, pairs, shards = sizes
    devices, _, rows, _ = received.shape
    ext_pieces, parts, columns, mixed_all = refs[:devices], refs[devices:-2], refs[-2], refs[-1]
    width = xn_all.shape[1]
    rows_each = width // shards
    for source in range(devices):
        for block in range(per):
            columns[source * rows : (source + 1) * rows, block * LANES : (block + 1) * LANES] = received[
                source, block
            ]

    def store(value, line):
        for owner in range(shards):
            for mask in range(shards):

                @pl.when(ids[1] ^ mask == owner)
                def _():
                    parts[mask][:rows_each, line] = value[
                        owner * rows_each : (owner + 1) * rows_each
                    ].astype(BF)

    step = per if 3 * pairs % per == 0 else 1
    for block in range(0, per, step):
        inside = ids[0] * per + block < 3 * pairs
        line = slice(block * LANES, (block + step) * LANES)

        @pl.when(inside)
        def _():
            store(dot(xn_all[...], columns[:, line], TN), line)

        @pl.when(jnp.logical_not(inside))
        def _():
            for mask, piece in enumerate(ext_pieces):
                start = pl.multiple_of((ids[0] ^ mask) * rows, rows)
                mixed_all[pl.ds(start, rows), :] = piece[:, :width]
            store(dot(mixed_all[...], columns[:, line], TN), line)

    for mask in range(shards):
        parts[mask][rows_each:, :] = lines[ids[1] ^ mask]


def spread_body(sizes, ids, *refs):
    per, pairs = sizes
    pieces, (in_grad, out_grad, router_grad, gain_one, gain_two, table_grad) = refs[:-6], refs[-6:]
    rows = in_grad.shape[0]
    total = None
    for mask, piece in enumerate(pieces):
        source = ids[0] ^ mask
        extra = piece[rows:, :].astype(F32)
        total = extra if total is None else total + extra
        for block in range(per):
            index = source * per + block
            values = piece[:rows, block * LANES : (block + 1) * LANES].astype(F32)

            @pl.when(index < 3 * pairs)
            def _():
                in_grad[:, pl.ds(pl.multiple_of(index * LANES, LANES), LANES)] = values

            @pl.when(jnp.logical_and(index >= 3 * pairs, index < 4 * pairs))
            def _():
                out_grad[:, pl.ds(pl.multiple_of((index - 3 * pairs) * LANES, LANES), LANES)] = values

    line_rows, span = total.shape
    line = 0
    for ref in (router_grad, gain_one, gain_two, table_grad):
        count, lanes = ref.shape
        group, row = divmod(line, line_rows)
        moved = pltpu.roll(total, span - group * rows, 1) if group else total
        ref[...] = moved[row : row + count, :lanes]
        line += count


def pad_to(x, shape):
    return jnp.pad(x, [(0, size - have) for size, have in zip(shape, x.shape)])


def local(
    tokens, gain_attn, gain_mix, attn_in, attn_out, router, bias_table, expert_in, expert_down, routes, buckets, out_grad
):
    own_tokens = tokens[0]
    own_grad = out_grad[0]
    rows, width = own_tokens.shape
    devices = lax.axis_size("expert")
    shards = lax.axis_size("wshard")
    expert_id = lax.axis_index("expert")
    shard_id = lax.axis_index("wshard")
    heads = bias_table.shape[1]
    head_dim = width // heads
    experts = router.shape[1]
    bucket_count = bias_table.shape[0] * shards
    per_device = expert_in.shape[0]
    keys = rows * devices
    capacity = 3 * rows // (2 * experts)
    part = width // shards
    ids = jnp.stack([expert_id, shard_id]).astype(jnp.int32)

    table_rows = bias_table.shape[0]
    head_rows = 16
    small = jnp.concatenate(
        [
            router,
            gain_attn[:, None],
            gain_mix[:, None],
            pad_to(bias_table, (part, LANES - experts - 2)),
        ],
        axis=1,
    )
    in_chunks = weight_chunks(attn_in, small)
    chip_tokens = chip_pieces(own_tokens)
    window_width = keys + rows
    start = keys - 1 - expert_id * rows - (rows - 1)
    window_buckets = lax.dynamic_slice(jnp.pad(buckets, (0, rows)), (start,), (window_width,))
    mirror_buckets = lax.dynamic_slice(jnp.pad(buckets[::-1], (0, rows)), (start,), (window_width,))
    last = jnp.arange(window_width) == window_width - 1
    window_buckets = jnp.where(last, -1, window_buckets)[None]
    mirror_buckets = jnp.where(last, -1, mirror_buckets)[None]

    route = routes[0]
    earlier = jnp.arange(rows)[None, :] < jnp.arange(rows)[:, None]
    rank = jnp.sum(((route[None, :] == route[:, None]) & earlier).astype(jnp.int32), axis=1)
    slot = route * capacity + rank
    slot_count = experts * capacity
    slots = (jnp.arange(slot_count)[:, None] == slot[None, :]).astype(BF)
    back_slots = (slot[:, None] == jnp.arange(slot_count)[None, :]).astype(BF)
    chosen = (route[:, None] == jnp.arange(LANES)[None, :]).astype(BF)

    block = per_device * capacity

    def exchange(slot_rows):
        blocks = slot_rows.reshape(devices, block, width)
        moved = lax.all_to_all(blocks, "expert", split_axis=0, concat_axis=0, tiled=True)
        return moved.reshape(devices * block, width)

    def sum_back(parts):
        total = parts[0].astype(F32)
        for mask in range(1, shards):
            total = total + swap(parts[mask], "wshard", mask).astype(F32)
        return total.astype(BF)

    chip_tokens, in_chunks, attn_out, ups = tie(
        chip_tokens, in_chunks, attn_out, dot(slots, own_grad).astype(BF)
    )
    in_pieces = in_chunks
    if len(in_chunks) > 1:
        in_pieces = chip_pieces(jnp.concatenate(in_chunks, axis=0))
    token_pieces = core_pieces(chip_tokens)
    first_step, *later_steps = doubling_steps(shards)
    w_rows = swap(attn_out, "wshard", first_step)
    in_pieces, token_pieces, w_rows, ups, ids, window_buckets, mirror_buckets, chosen, slots, back_slots = tie(
        in_pieces,
        token_pieces,
        w_rows,
        exchange(ups),
        ids,
        window_buckets,
        mirror_buckets,
        chosen,
        slots,
        back_slots,
    )
    w_rows = jnp.concatenate([attn_out, w_rows], axis=0)
    for step in later_steps:
        w_rows = jnp.concatenate([w_rows, swap(w_rows, "wshard", step)], axis=0)
    ups_far = swap(ups, "wshard", first_step)
    if len(in_pieces) > 1:
        in_pieces = core_pieces(in_pieces)

    sizes = (devices, shards, heads, head_dim, bucket_count, experts, len(in_pieces))
    xn_all, joined, joined_own, ext, window, mirror, gains, router_pad = call(
        functools.partial(forward_body, sizes),
        [ids, *token_pieces, *in_pieces, window_buckets, mirror_buckets],
        [
            ((keys, width), BF),
            ((keys, 3 * width), BF),
            ((rows, 3 * width), BF),
            ((rows, width + LANES), BF),
            ((head_rows, window_width), F32),
            ((head_rows, window_width), F32),
            ((8, width), F32),
            ((width, LANES), BF),
        ],
        [
            pltpu.VMEM((keys, width), BF),
            pltpu.VMEM((keys, 3 * width), BF),
            pltpu.VMEM((width, 3 * width), BF),
            pltpu.SemaphoreType.DMA((2,)),
        ],
        far=(0, 1),
        name="attention_forward",
        us=0.2,
    )
    ups_far, w_rows, ext = tie(ups_far, w_rows, ext)
    ups_all = jnp.concatenate([ups, ups_far], axis=0)
    for step in later_steps:
        ups_all = jnp.concatenate([ups_all, swap(ups_all, "wshard", step)], axis=0)
    after, gate, send, w_out = call(
        functools.partial(route_body, (experts, shards)),
        [ids, w_rows, own_tokens, ext, gains, router_pad, chosen, slots],
        [((rows, width), F32), ((rows, LANES), F32), ((slot_count, width), BF), ((width, width), BF)],
        name="route",
        us=0.2,
    )
    rows_own = exchange(send)
    total = devices * block
    count = total // per_device
    ff = expert_in.shape[2]
    by_expert = pl.BlockSpec((1, width, ff), lambda k: (k, 0, 0))
    kept_ff = pl.BlockSpec((1, count, ff), lambda k: (k, 0, 0))
    kept_width = pl.BlockSpec((1, count, width), lambda k: (k, 0, 0))
    kept_lanes = pl.BlockSpec((1, count, LANES), lambda k: (k, 0, 0))
    upstream_width = pl.BlockSpec((1, shards * count, width), lambda k: (k, 0, 0))
    upstream_ff = pl.BlockSpec((1, shards * count, ff), lambda k: (k, 0, 0))
    ups_all, rows_own = tie(ups_all, rows_own)
    row_chunks = {0: rows_own}
    steps = [1 << bit for bit in reversed(range((shards - 1).bit_length()))]
    row_chunks.update({step: swap(rows_own, "wshard", step) for step in steps})
    ups_all, spread_all = pl.pallas_call(
        functools.partial(upstream_body, (shards, per_device, capacity)),
        grid=(per_device,),
        in_specs=[whole((shards * total, width)), by_expert],
        out_specs=[upstream_width, upstream_ff],
        out_shape=[
            jax.ShapeDtypeStruct((per_device, shards * count, width), BF),
            jax.ShapeDtypeStruct((per_device, shards * count, ff), F32),
        ],
        compiler_params=pltpu.CompilerParams(vmem_limit_bytes=VMEM_BYTES),
        cost_estimate=cost(0.001),
        name="upstream",
    )(ups_all, expert_down)
    ext_later, _ = tie(ext, rows_own)
    ext_chips = chip_pieces(ext_later)
    kept = [[], [], [], [], []]
    back_parts = []
    for step in range(shards):
        row_chunk = row_chunks[step]
        if step:
            row_chunk, _ = tie(row_chunk, back_parts[-1])
        if step == shards - 1:
            row_chunk, ext_chips = tie(row_chunk, ext_chips)
            ext_pieces = core_pieces(ext_chips)
        back, *saved = pl.pallas_call(
            functools.partial(expert_body, (experts, per_device, capacity)),
            grid=(per_device,),
            in_specs=[
                pl.BlockSpec(memory_space=pltpu.SMEM),
                whole((total, width)),
                pl.BlockSpec((1, count, width), lambda k, step=step: (k, step, 0)),
                pl.BlockSpec((1, count, ff), lambda k, step=step: (k, step, 0)),
                by_expert,
                whole((width, LANES)),
            ],
            out_specs=[whole((total, width)), kept_width, kept_width, kept_ff, kept_ff, kept_lanes],
            out_shape=[
                jax.ShapeDtypeStruct((total, width), BF),
                jax.ShapeDtypeStruct((per_device, count, width), BF),
                jax.ShapeDtypeStruct((per_device, count, width), BF),
                jax.ShapeDtypeStruct((per_device, count, ff), BF),
                jax.ShapeDtypeStruct((per_device, count, ff), BF),
                jax.ShapeDtypeStruct((per_device, count, LANES), F32),
            ],
            compiler_params=pltpu.CompilerParams(vmem_limit_bytes=VMEM_BYTES),
            cost_estimate=cost(0.001),
            name="experts",
        )(ids, row_chunk, ups_all, spread_all, expert_in, router_pad)
        back_parts.append(back)
        for group, value in zip(kept, saved):
            group.append(value)
        if step == 1:
            for mask in range(1, shards):
                nearer = mask & (-mask)
                if mask != nearer:
                    value, _ = tie(row_chunks[mask ^ nearer], back)
                    row_chunks[mask] = swap(value, "wshard", nearer)
    kept, back_sum, ext_pieces = tie(kept, sum_back(back_parts), ext_pieces)
    returned_grad = exchange(back_sum)
    out_near, out_far, router_part = pl.pallas_call(
        functools.partial(expert_out_body, (shards, per_device, capacity)),
        grid=(per_device,),
        in_specs=[kept_width] * shards + [kept_ff] * shards + [kept_lanes] * shards + [by_expert],
        out_specs=[whole((shards // 2 * total, width))] * 2 + [whole((LANES, width))],
        out_shape=[jax.ShapeDtypeStruct((shards // 2 * total, width), BF)] * 2
        + [jax.ShapeDtypeStruct((LANES, width), F32)],
        compiler_params=pltpu.CompilerParams(vmem_limit_bytes=VMEM_BYTES),
        cost_estimate=cost(5.0),
        name="expert_out",
    )(*kept[0], *kept[2], *kept[4], expert_down)
    out_near, out_far, router_part, returned_grad = tie(out_near, out_far, router_part, returned_grad)
    out_sum = (out_near.astype(F32) + swap(out_far, "wshard", 1).astype(F32)).astype(BF)
    resid, resid_low, grad_ext, gain_two_part = call(
        functools.partial(residual_body, (heads, head_dim)),
        [ids, returned_grad, back_slots, after, own_grad, gains, ext, w_out],
        [((rows, width), F32), ((rows, width), BF), ((rows, width + LANES), BF), ((1, width), F32)],
        name="residual",
        us=2.0,
    )
    grad_pieces = chip_pieces(grad_ext)
    pairs = heads // 2

    def column_block(offset):
        return pl.BlockSpec((keys, LANES), lambda p: (0, offset * pairs + p))

    query_grad, table_part = pl.pallas_call(
        functools.partial(query_body, (head_dim, bucket_count)),
        grid=(pairs,),
        in_specs=[
            pl.BlockSpec(memory_space=pltpu.SMEM),
            whole((rows, width + LANES)),
            whole((rows, width + LANES)),
            whole((rows, 3 * width)),
            whole((head_rows, window_width)),
            whole((1, window_width)),
            column_block(1),
            column_block(2),
        ],
        out_specs=[pl.BlockSpec((1, rows, LANES), lambda p: (p, 0, 0)), whole((head_rows, bucket_count))],
        out_shape=[
            jax.ShapeDtypeStruct((pairs, rows, LANES), BF),
            jax.ShapeDtypeStruct((head_rows, bucket_count), F32),
        ],
        scratch_shapes=[
            pltpu.VMEM((rows, head_rows), F32),
            pltpu.VMEM((rows, head_rows), F32),
            pltpu.VMEM((head_rows * 8, window_width), F32),
        ],
        compiler_params=pltpu.CompilerParams(vmem_limit_bytes=VMEM_BYTES),
        cost_estimate=cost(10.0),
        name="query_grad",
    )(ids, grad_ext, ext, joined_own, window, window_buckets, joined, joined)
    per = -(-4 * pairs // devices)
    grad_pieces, query_grad = tie(grad_pieces, query_grad)
    grad_pieces = core_pieces(grad_pieces)
    (blocks,) = pl.pallas_call(
        functools.partial(key_body, (devices, heads, head_dim)),
        grid=(pairs,),
        in_specs=[pl.BlockSpec(memory_space=pltpu.SMEM)]
        + [whole((rows, width + LANES))] * (2 * devices)
        + [
            whole((rows, 3 * width)),
            whole((head_rows, window_width)),
            whole((pairs, rows, LANES)),
            whole((rows, width)),
            column_block(0),
        ],
        out_specs=[whole((per * devices, rows, LANES))],
        out_shape=[
            jax.ShapeDtypeStruct((per * devices, rows, LANES), BF),
        ],
        scratch_shapes=[
            pltpu.VMEM((keys, width + LANES), BF),
            pltpu.VMEM((head_rows, keys), F32),
            pltpu.VMEM((head_rows, keys), F32),
        ],
        compiler_params=pltpu.CompilerParams(vmem_limit_bytes=VMEM_BYTES),
        cost_estimate=cost(12.0),
        name="key_grad",
    )(ids, *grad_pieces, *ext_pieces, joined_own, mirror, query_grad, resid_low, joined)
    *nearer_steps, far_step = reversed(doubling_steps(shards)[:-1])
    for step in nearer_steps:
        half = out_sum.shape[0] // 2
        moved = swap(out_sum[half:], "wshard", step)
        out_sum = (out_sum[:half].astype(F32) + moved.astype(F32)).astype(BF)
    out_moved = swap(out_sum[out_sum.shape[0] // 2 :], "wshard", far_step)
    received = lax.all_to_all(
        blocks.reshape(devices, per, rows, LANES), "expert", split_axis=0, concat_axis=0, tiled=True
    )
    tokens_grad, gain_one_part = call(
        functools.partial(source_body, shards),
        [ids, blocks, own_tokens, gains, resid, *in_pieces],
        [((rows, width), BF), ((1, width), F32)],
        [
            pltpu.VMEM((rows, 3 * width), BF),
            pltpu.VMEM((width, 3 * width), BF),
            pltpu.VMEM((width, LANES), BF),
        ],
        name="source_grad",
        us=4.0,
    )
    table_lines = table_part[:heads].reshape(heads, shards, table_rows)
    table_lines = pad_to(table_lines, (heads, shards, part)).reshape(heads, width)
    lines = jnp.concatenate([router_part[:experts], gain_one_part, gain_two_part, table_lines], axis=0)
    line_count = lines.shape[0]
    groups = per * LANES // part
    line_rows = -(-line_count // (16 * groups)) * 16
    lines = pad_to(lines, (groups * line_rows, width)).reshape(groups, line_rows, shards, part)
    lines = lines.transpose(2, 1, 0, 3).reshape(shards, line_rows, groups * part)
    lines = pad_to(lines, (shards, line_rows, per * LANES)).astype(BF)
    weight_parts = call(
        functools.partial(weight_body, (per, pairs, shards)),
        [ids, xn_all, received, lines, *ext_pieces],
        [((part + line_rows, per * LANES), BF)] * shards,
        [pltpu.VMEM((keys, per * LANES), BF), pltpu.VMEM((keys, width), BF)],
        name="weight_grads",
        us=4.0,
    )
    weight_parts, kept = tie(weight_parts, kept)
    up_grad, down_grad = pl.pallas_call(
        functools.partial(expert_weights_body, shards),
        grid=(per_device,),
        in_specs=[kept_width] * (2 * shards) + [kept_ff] * (2 * shards),
        out_specs=[by_expert, by_expert],
        out_shape=[jax.ShapeDtypeStruct((per_device, width, ff), F32)] * 2,
        compiler_params=pltpu.CompilerParams(vmem_limit_bytes=VMEM_BYTES),
        cost_estimate=cost(7.0),
        name="expert_weights",
    )(*kept[0], *kept[1], *kept[2], *kept[3])
    mine = sum_back(weight_parts)
    mine, out_moved, up_grad, down_grad = tie(mine, out_moved, up_grad, down_grad)
    pieces, out_moved = tie(chip_pieces(mine), out_moved)
    out_sum = (out_sum[: out_moved.shape[0]].astype(F32) + out_moved.astype(F32)).astype(BF)
    returned_rows = exchange(out_sum)
    (result,) = call(
        result_body,
        [ids, returned_rows, back_slots, after, gate],
        [((rows, width), BF)],
        name="result",
        us=2.0,
    )
    attn_in_grad, attn_out_grad, router_grad, gain_one_grad, gain_two_grad, table_grad = call(
        functools.partial(spread_body, (per, pairs)),
        [ids, *core_pieces(pieces)],
        [
            ((part, 3 * width), F32),
            ((part, width), F32),
            ((experts, part), F32),
            ((1, part), F32),
            ((1, part), F32),
            ((heads, table_rows), F32),
        ],
        name="spread",
        us=2.0,
    )
    return (
        result[None],
        tokens_grad[None],
        gain_one_grad[0],
        gain_two_grad[0],
        attn_in_grad,
        attn_out_grad,
        router_grad.T,
        table_grad.T,
        up_grad,
        down_grad,
    )


def solution(mesh):
    return jax.shard_map(
        local,
        mesh=mesh,
        in_specs=(
            P("wshard", "expert", None),
            P("wshard"),
            P("wshard"),
            P("wshard", None),
            P("wshard", None),
            P("wshard", None),
            P("wshard", None),
            P("expert", None, "wshard"),
            P("expert", None, "wshard"),
            P("wshard", "expert"),
            P(),
            P("wshard", "expert", None),
        ),
        out_specs=(
            P("wshard", "expert", None),
            P("wshard", "expert", None),
            P("wshard"),
            P("wshard"),
            P("wshard", None),
            P("wshard", None),
            P("wshard", None),
            P("wshard", None),
            P("expert", None, "wshard"),
            P("expert", None, "wshard"),
        ),
        check_vma=False,
    )
```
